256 devices in a mesh: rows: 16 (over z_lo, y, core), near: 4 (over z_hi), far: 4 (over x).
Axes of the slice: x: 4, y: 4, z: 8 (z_hi: 4, z_lo: 2; z = z_hi * 2 + z_lo), core: 2. Of those that a mesh axis runs over, the one named last changes fastest.
Arguments:
- diag_block: float32 [512, 512], replicated, as said below
- history_rows: float32 [512, 24576], P('rows', ('near', 'far'))
- panel_below: float32 [16384, 512], P(('rows', 'near', 'far')), may hold values from -6 to 6
- history_below: float32 [16384, 24576], P('rows', ('near', 'far')), may hold values from -6 to 6
Outputs:
- panel_factor: float32 [16384, 512], P(('rows', 'near', 'far'))
- diag_factor: float32 [512, 512], replicated
The draws below stay inside these ranges and needn't reach their ends.
Inputs may be any that keep to these rules, and one draw needn't show every extreme that they name: diag_block minus history_rows history_rows^T is symmetric with a dominant positive diagonal.
All inputs are finite; a program needn't handle non-finite values.
Results may differ from the reference program's by a relative error of at most 0.000067.
Values sent between devices are 32-bit elements; how exact they have to be, the bound alone decides.
No kernel may reach another device: no remote copies, remote signals or barrier semaphores. Data moves between devices by JAX's collectives and lax.ppermute only.
A program may use at most 64 MiB of HBM per device.

```python
import math
import jax
import jax.numpy as jnp
from jax import lax

PANEL = 512
ROWS_ALL = 16384
HIST = 24576


def history_draw(key):
    base = jax.random.normal(key, (PANEL, HIST), jnp.float32)
    return base / math.sqrt(HIST)


def draw_history_rows(key, part):
    return history_draw(key)


def draw_diag_block(key, part):
    shared = history_draw(key)
    key = jax.random.fold_in(key, 7)
    key_off, key_diag = jax.random.split(key)
    product = jnp.dot(shared, shared.T, precision=lax.Precision.HIGHEST)
    off = jax.random.uniform(key_off, (PANEL, PANEL), jnp.float32, -1.0, 1.0) / PANEL
    off = off + off.T
    diagonal = jax.random.uniform(key_diag, (PANEL,), jnp.float32, 1.5, 3.0)
    return product + off * (1.0 - jnp.eye(PANEL, dtype=jnp.float32)) + jnp.diag(diagonal)


def with_spikes(array, rng, source, target, parts, factor):
    owner, partner = [(jnp.arange(array.shape[axis_at]) // (array.shape[axis_at] // parts)).reshape([-1 if axis == axis_at else 1 for axis in range(array.ndim)]) for axis_at in (source, target)]
    chosen = jax.random.permutation(rng, parts)[partner]
    strong = (owner == chosen) | (owner == (partner + parts // 2) % parts)
    return jnp.where(strong, factor * array, array)


def block_scale(own_key, shape, cuts, smallest, top_value):
    factor_of, own = 1.0, jax.random.fold_in(own_key, 6)
    for axis_at, parts in cuts:
        draws = jnp.exp(jax.random.uniform(jax.random.fold_in(own, axis_at), (parts,), jnp.float32, smallest / len(cuts), top_value / len(cuts)))
        factor_of = factor_of * jnp.repeat(draws, shape[axis_at] // parts).reshape([-1 if axis == axis_at else 1 for axis in range(len(shape))])
    return factor_of


def scatter_about(stream_key, dims, width, limit, cuts=(), held_as=jnp.bfloat16):
    array = jax.random.normal(stream_key, dims, jnp.float32) * width
    if len(cuts) > 0:
        array = block_scale(stream_key, dims, cuts, -0.22, 0.18) * array
    return jnp.clip(array, min=-limit, max=limit).astype(held_as)


def noise_with(stream_key, shape, scale, bound, pieces, heavy, kind=jnp.bfloat16):
    array = scale * jax.random.normal(stream_key, shape, jnp.float32)
    if pieces:
        array = array * block_scale(stream_key, shape, pieces, -0.22, 0.18)
    return jnp.clip(with_spikes(array, jax.random.fold_in(stream_key, 3), *heavy), -bound, bound).astype(kind)


def setup_inputs(seed: int = 0) -> dict:
    arg_keys = jax.random.split(jax.random.key(seed), 5)
    diag_block = draw_diag_block(jax.random.fold_in(arg_keys[4], 71), 0)
    history_rows = draw_history_rows(jax.random.fold_in(arg_keys[4], 71), 0)
    panel_below = scatter_about(arg_keys[2], (ROWS_ALL, PANEL), 1.0, 6.0, ((0, 256),), jnp.float32)
    history_below = noise_with(arg_keys[3], (ROWS_ALL, HIST), 1.0, 6.0, ((0, 16), (1, 16)), (1, 0, 16, 2.0), jnp.float32)
    return dict(diag_block=diag_block, history_rows=history_rows, panel_below=panel_below, history_below=history_below)


def reference(diag_block, history_rows, panel_below, history_below):
    highest = lax.Precision.HIGHEST
    schur = diag_block - jnp.dot(history_rows, history_rows.T, precision=highest)
    diag_factor = jnp.linalg.cholesky(schur)
    identity = jnp.eye(PANEL, dtype=jnp.float32)
    inverse = lax.linalg.triangular_solve(diag_factor, identity, left_side=True, lower=True)
    updated = panel_below - jnp.dot(history_below, history_rows.T, precision=highest)
    panel_factor = jnp.dot(updated, inverse.T, precision=highest)
    return (panel_factor, diag_factor)
```

```python
import functools

import jax
import jax.numpy as jnp
from jax import lax
from jax.experimental import pallas as pl
from jax.experimental.pallas import tpu as pltpu
from jax.sharding import PartitionSpec as P

F32, BF16 = jnp.float32, jnp.bfloat16
NT = (((1,), (1,)), ((), ()))
NN = (((1,), (0,)), ((), ()))
VMEM = pl.BlockSpec(memory_space=pltpu.VMEM)
SMEM = pl.BlockSpec(memory_space=pltpu.SMEM)


def split(x):
    hi = x.astype(BF16)
    return hi, (x - hi.astype(F32)).astype(BF16)


def dot3(a, b, dims):
    d = lambda x, y: lax.dot_general(x, y, dims, preferred_element_type=F32)
    return d(a[0], b[1]) + d(a[1], b[0]) + d(a[0], b[0])


def call(kernel, out_shape, in_specs, args, scratch=(), flops=0, moved=0):
    outs = jax.tree.map(lambda _: VMEM, out_shape)
    return pl.pallas_call(
        kernel,
        out_shape=out_shape,
        in_specs=in_specs,
        out_specs=outs,
        scratch_shapes=list(scratch),
        cost_estimate=pl.CostEstimate(flops=flops, bytes_accessed=moved, transcendentals=0),
        compiler_params=pltpu.CompilerParams(vmem_limit_bytes=40 * 1024 * 1024),
    )(*args)


def place(me, y_step, z_step, core_step):
    return me ^ (y_step * 2 + z_step * 8 + core_step)


def assemble_kernel(me_ref, *refs):
    pieces, (hi_ref, lo_ref, schur_ref) = refs[:8], refs[8:]
    me = me_ref[0]
    size = pieces[0].shape[0] // 2
    own = split(pieces[0][:size, :])
    for core_step in range(2):
        for y_step in range(4):
            piece = pieces[core_step * 4 + y_step]
            for z_step in range(2):
                at = pl.ds(pl.multiple_of(place(me, y_step, z_step, core_step) * size, size), size)
                hi, lo = split(piece[z_step * size:(z_step + 1) * size, :])
                hi_ref[at, :] = hi
                lo_ref[at, :] = lo
    schur_ref[...] = dot3(own, (hi_ref[...], lo_ref[...]), NT)


def product_kernel(at_ref, b0, b1, b2, b3, hi_ref, lo_ref, out_ref):
    rows = jnp.concatenate([b[0, 0] for b in (b0, b1, b2, b3)], 0)
    out_ref[...] = dot3(split(rows), (hi_ref[...], lo_ref[...]), NT)


def product(at, step, below, hi, lo):
    near_n, far_n, share, depth = below.shape
    panel = hi.shape[0]
    spec = lambda j: pl.BlockSpec((1, 1, share, depth), lambda i, at: (at[0] ^ j, at[1] ^ step, 0, 0))
    whole = pl.BlockSpec((panel, depth), lambda i, at: (0, 0))
    return pl.pallas_call(
        product_kernel,
        out_shape=jax.ShapeDtypeStruct((near_n * share, panel), F32),
        grid_spec=pltpu.PrefetchScalarGridSpec(
            num_scalar_prefetch=1,
            grid=(1,),
            in_specs=[spec(j) for j in range(near_n)] + [whole, whole],
            out_specs=pl.BlockSpec((near_n * share, panel), lambda i, at: (0, 0)),
        ),
        cost_estimate=pl.CostEstimate(
            flops=6 * near_n * share * depth * panel, bytes_accessed=6 * 2**20, transcendentals=0),
        compiler_params=pltpu.CompilerParams(vmem_limit_bytes=40 * 1024 * 1024),
    )(at, below, below, below, below, hi, lo)


def recip(x):
    r = pl.reciprocal(x, approx=True)
    return r * (2.0 - x * r)


def factor_block(rows, nb):
    groups = len(rows)
    lane = lax.broadcasted_iota(jnp.int32, (8, nb), 1)
    sub = lax.broadcasted_iota(jnp.int32, (8, nb), 0)
    rows = list(rows)
    inv = [jnp.where(lane == sub + 8 * g, 1.0, 0.0) for g in range(groups)]
    bc = lambda x, k: jnp.broadcast_to(x[k:k + 1, :], (8, nb))
    for t in range(groups):
        cols = {
            g: [jnp.broadcast_to(rows[g][:, 8 * t + k:8 * t + k + 1], (8, nb)) for k in range(8)]
            for g in range(t, groups)
        }
        diag = jnp.ones((8, nb), F32)
        for k in range(8):
            piv = bc(cols[t][k], k)
            diag = jnp.where(sub == k, piv, diag)
            r = recip(piv)
            if k < 7 or t < groups - 1:
                bcols = {m: bc(cols[t][m], k) for m in range(k + 1, 8)}
                brow = bc(rows[t], k)
                binv = bc(inv[t], k)
                for g in range(t, groups):
                    f = cols[g][k] * r
                    if g == t:
                        f = jnp.where(sub > k, f, 0.0)
                    for m in range(k + 1, 8):
                        cols[g][m] = cols[g][m] - f * bcols[m]
                    rows[g] = rows[g] - f * brow
                    inv[g] = inv[g] - f * binv
        scale = lax.rsqrt(diag)
        rows[t] = jnp.where(lane >= sub + 8 * t, rows[t] * scale, 0.0)
        inv[t] = inv[t] * scale
    return rows, inv


def cholesky_kernel(me_ref, diag_ref, *refs):
    pieces, (l_ref, x_ref, w_ref) = refs[:8], refs[8:]
    me = me_ref[0]
    size = pieces[0].shape[0] // 2
    for core_step in range(2):
        for y_step in range(4):
            piece = pieces[core_step * 4 + y_step]
            for z_step in range(2):
                at = pl.ds(pl.multiple_of(place(me, y_step, z_step, core_step) * size, size), size)
                w_ref[at, :] = diag_ref[at, :] - piece[z_step * size:(z_step + 1) * size, :]
    n = diag_ref.shape[0]
    nb = 128
    steps = n // nb
    blk = lambda i: slice(i * nb, (i + 1) * nb)
    l_ref[...] = jnp.zeros_like(l_ref)
    x_ref[...] = jnp.zeros_like(x_ref)
    for b in range(steps):
        rows = [w_ref[b * nb + 8 * g:b * nb + 8 * g + 8, blk(b)] for g in range(nb // 8)]
        up, inv = factor_block(rows, nb)
        x11 = jnp.concatenate(inv, 0)
        l_ref[blk(b), blk(b)] = jnp.concatenate(up, 0).T
        x_ref[blk(b), blk(b)] = x11
        if b + 1 < steps:
            rest = slice((b + 1) * nb, n)
            l21 = dot3(split(w_ref[rest, blk(b)]), split(x11), NT)
            l_ref[rest, blk(b)] = l21
            ls = split(l21)
            w_ref[rest, rest] = w_ref[rest, rest] - dot3(ls, ls, NT)
        if b > 0:
            done = slice(0, b * nb)
            t = dot3(split(l_ref[blk(b), done]), split(x_ref[done, done]), NN)
            x_ref[blk(b), done] = -dot3(split(x11), split(t), NN)


def final_kernel(below_ref, p0, p1, p2, p3, x_ref, out_ref):
    updated = below_ref[...] - ((p0[...] + p1[...]) + (p2[...] + p3[...]))
    out_ref[...] = dot3(split(updated), split(x_ref[...]), NT)


def swap(x, axis, size, step):
    return lax.ppermute(x, axis, [(i, i ^ step) for i in range(size)])


def tree(a, b, c, d):
    return (a + b) + (c + d)


def gather_rows(x, size):
    pair = jnp.concatenate([x, swap(x, "rows", size, 8)], 0)
    mine = [pair] + [swap(pair, "rows", size, 2 * k) for k in (1, 2, 3)]
    return mine + [swap(p, "rows", size, 1) for p in mine]


def body(sizes, diag_block, history_rows, panel_below, history_below):
    rows_n, near_n, far_n = sizes
    panel = diag_block.shape[0]
    mine, depth = history_rows.shape
    share = panel_below.shape[0]
    me = lax.axis_index("rows").reshape(1)
    at = jnp.stack([lax.axis_index("near"), lax.axis_index("far")])
    pieces = gather_rows(history_rows, rows_n)
    gathered = jax.ShapeDtypeStruct((panel, depth), BF16)
    hi, lo, schur_part = call(
        assemble_kernel,
        (gathered, gathered, jax.ShapeDtypeStruct((mine, panel), F32)),
        [SMEM] + [VMEM] * 8,
        [me] + pieces,
        flops=6 * mine * depth * panel,
        moved=12 * panel * depth,
    )
    for axis, size in (("far", far_n), ("near", near_n)):
        schur_part = tree(schur_part, *[swap(schur_part, axis, size, k) for k in (1, 2, 3)])
    schur_pieces = gather_rows(schur_part, rows_n)
    below = history_below.reshape(near_n, far_n, share, depth)
    parts = [product(at, k, below, hi, lo) for k in (0, 1, 2, 3)]
    parts = [parts[0]] + [swap(parts[k], "far", far_n, k) for k in (1, 2, 3)]
    quarter = lambda p, j: p[j * share:(j + 1) * share]
    sums = [tree(*[quarter(p, j) for p in parts]) for j in range(near_n)]
    sums = [sums[0]] + [swap(sums[j], "near", near_n, j) for j in (1, 2, 3)]
    square = jax.ShapeDtypeStruct((panel, panel), F32)
    diag_factor, inverse = call(
        cholesky_kernel,
        (square, square),
        [SMEM] + [VMEM] * 9,
        [me, diag_block] + schur_pieces,
        scratch=[pltpu.VMEM((panel, panel), F32)],
        flops=2 * panel**3,
        moved=16 * panel * panel,
    )
    panel_factor = call(
        final_kernel,
        jax.ShapeDtypeStruct((share, panel), F32),
        [VMEM] * 6,
        [panel_below] + sums + [inverse],
        flops=6 * share * panel * panel,
        moved=8 * panel * panel,
    )
    return (panel_factor, diag_factor)


def solution(mesh):
    sizes = tuple(mesh.shape[name] for name in ("rows", "near", "far"))
    return jax.shard_map(
        functools.partial(body, sizes),
        mesh=mesh,
        in_specs=(
            P(),
            P("rows", ("near", "far")),
            P(("rows", "near", "far"), None),
            P("rows", ("near", "far")),
        ),
        out_specs=(P(("rows", "near", "far"), None), P()),
        check_vma=False,
    )
```

```python
import functools

import jax
import jax.numpy as jnp
from jax import lax
from jax.experimental import pallas as pl
from jax.experimental.pallas import tpu as pltpu
from jax.sharding import PartitionSpec as P

F32, BF16 = jnp.float32, jnp.bfloat16
NT = (((1,), (1,)), ((), ()))
NN = (((1,), (0,)), ((), ()))
VMEM = pl.BlockSpec(memory_space=pltpu.VMEM)
SMEM = pl.BlockSpec(memory_space=pltpu.SMEM)


def split(x):
    hi = x.astype(BF16)
    return hi, (x - hi.astype(F32)).astype(BF16)


def dot3(a, b, dims):
    d = lambda x, y: lax.dot_general(x, y, dims, preferred_element_type=F32)
    return d(a[0], b[1]) + d(a[1], b[0]) + d(a[0], b[0])


def call(kernel, out_shape, in_specs, args, scratch=(), flops=0, moved=0, vmem=16):
    outs = jax.tree.map(lambda _: VMEM, out_shape)
    return pl.pallas_call(
        kernel,
        out_shape=out_shape,
        in_specs=in_specs,
        out_specs=outs,
        scratch_shapes=list(scratch),
        cost_estimate=pl.CostEstimate(flops=flops, bytes_accessed=moved, transcendentals=0),
        compiler_params=pltpu.CompilerParams(vmem_limit_bytes=vmem * 2**20),
    )(*args)


def at_rows(me, z, y_step, core_step, size):
    place = z * 8 + lax.rem(me ^ (y_step * 2 + core_step), 8)
    return pl.ds(pl.multiple_of(place * size, size), size)


def slot_of(shape, size):
    return lax.rem(lax.broadcasted_iota(jnp.int32, shape, 1) // (2 * size), 4)


def schur_kernel(me_ref, *refs):
    pieces, (out_ref, hi_ref, lo_ref) = refs[:6], refs[6:]
    me = me_ref[0]
    size = pieces[0].shape[0] // 2
    for core_step in range(2):
        for i, y_step in enumerate((0, 1, 3)):
            hi, lo = split(pieces[core_step * 3 + i][...])
            for z in range(2):
                part = slice(z * size, (z + 1) * size)
                for slot in (y_step, 2) if y_step == 3 else (y_step,):
                    at = at_rows(me, z, slot, core_step, size)
                    hi_ref[at, :] = hi[part]
                    lo_ref[at, :] = lo[part]
    left = split(jnp.concatenate([pieces[0][...], pieces[1][...]], 0))
    both = dot3(left, (hi_ref[...], lo_ref[...]), NT)
    here, near = both[:2 * size], both[2 * size:]
    y = lax.rem(me // 2, 4)
    out_ref[...] = jnp.where(slot_of(here.shape, size) == (y ^ 2), near, here)


def assemble_kernel(me_ref, *refs):
    pieces, (hi_ref, lo_ref) = refs[:10], refs[10:]
    me = me_ref[0]
    size = pieces[0].shape[0] // 2
    for core_step in range(2):
        own = pieces[core_step * 5:core_step * 5 + 5]
        for y_step in range(4):
            for z in range(2):
                part = slice(z * size, (z + 1) * size)
                x = own[3 + z][...] if y_step == 2 else own[(0, 1, None, 2)[y_step]][part, :]
                hi, lo = split(x)
                at = at_rows(me, z, y_step, core_step, size)
                hi_ref[at, :] = hi
                lo_ref[at, :] = lo


def product_kernel(step, at_ref, below_ref, hi_ref, lo_ref, out_ref):
    near, far = at_ref[0], at_ref[1] ^ step
    rows = jnp.concatenate([below_ref[near ^ j, far] for j in range(below_ref.shape[0])], 0)
    out_ref[...] = dot3(split(rows), (hi_ref[...], lo_ref[...]), NT)


def product(at, step, below, hi, lo):
    near_n, far_n, share, depth = below.shape
    panel = hi.shape[0]
    return call(
        functools.partial(product_kernel, step),
        jax.ShapeDtypeStruct((near_n * share, panel), F32),
        [SMEM] + [VMEM] * 3,
        [at, below, hi, lo],
        flops=6 * near_n * share * depth * panel,
        moved=6 * 2**20,
    )


def recip(x):
    r = pl.reciprocal(x, approx=True)
    return r * (2.0 - x * r)


def factor_block(rows, nb):
    groups = len(rows)
    lane = lax.broadcasted_iota(jnp.int32, (8, nb), 1)
    sub = lax.broadcasted_iota(jnp.int32, (8, nb), 0)
    rows = list(rows)
    inv = [jnp.where(lane == sub + 8 * g, 1.0, 0.0) for g in range(groups)]
    bc = lambda x, k: jnp.broadcast_to(x[k:k + 1, :], (8, nb))
    for t in range(groups):
        cols = {
            g: [jnp.broadcast_to(rows[g][:, 8 * t + k:8 * t + k + 1], (8, nb)) for k in range(8)]
            for g in range(t, groups)
        }
        diag = jnp.ones((8, nb), F32)
        for k in range(8):
            piv = bc(cols[t][k], k)
            diag = jnp.where(sub == k, piv, diag)
            r = recip(piv)
            if k < 7 or t < groups - 1:
                bcols = {m: bc(cols[t][m], k) for m in range(k + 1, 8)}
                brow = bc(rows[t], k)
                binv = bc(inv[t], k)
                for g in range(t, groups):
                    f = cols[g][k] * r
                    if g == t:
                        f = jnp.where(sub > k, f, 0.0)
                    for m in range(k + 1, 8):
                        cols[g][m] = cols[g][m] - f * bcols[m]
                    rows[g] = rows[g] - f * brow
                    inv[g] = inv[g] - f * binv
        scale = lax.rsqrt(diag)
        rows[t] = jnp.where(lane >= sub + 8 * t, rows[t] * scale, 0.0)
        inv[t] = inv[t] * scale
    return rows, inv


def cholesky_kernel(me_ref, diag_ref, *refs):
    pieces, (l_ref, x_ref, w_ref) = refs[:8], refs[8:]
    me = me_ref[0]
    size = pieces[0].shape[0] // 2
    y = lax.rem(me // 2, 4)
    for core_step in range(2):
        for y_step in range(4):
            own = pieces[core_step * 4 + y_step][...]
            other = pieces[core_step * 4 + (y_step ^ 1)][...]
            tiles = [other[:, i:i + 128] for i in range(0, other.shape[1], 128)]
            other = jnp.concatenate([pltpu.roll(t, 64, 1) for t in tiles], 1)
            whole = jnp.where(slot_of(own.shape, size) == (y ^ y_step ^ 2), other, own)
            for z in range(2):
                at = at_rows(me, z, y_step, core_step, size)
                w_ref[at, :] = diag_ref[at, :] - whole[z * size:(z + 1) * size]
    n = diag_ref.shape[0]
    nb = 128
    steps = n // nb
    blk = lambda i: slice(i * nb, (i + 1) * nb)
    l_ref[...] = jnp.zeros_like(l_ref)
    x_ref[...] = jnp.zeros_like(x_ref)
    for b in range(steps):
        rows = [w_ref[b * nb + 8 * g:b * nb + 8 * g + 8, blk(b)] for g in range(nb // 8)]
        up, inv = factor_block(rows, nb)
        x11 = jnp.concatenate(inv, 0)
        l_ref[blk(b), blk(b)] = jnp.concatenate(up, 0).T
        x_ref[blk(b), blk(b)] = x11
        if b + 1 < steps:
            rest = slice((b + 1) * nb, n)
            l21 = dot3(split(w_ref[rest, blk(b)]), split(x11), NT)
            l_ref[rest, blk(b)] = l21
            ls = split(l21)
            w_ref[rest, rest] = w_ref[rest, rest] - dot3(ls, ls, NT)
        if b > 0:
            done = slice(0, b * nb)
            t = dot3(split(l_ref[blk(b), done]), split(x_ref[done, done]), NN)
            x_ref[blk(b), done] = -dot3(split(x11), split(t), NN)


def final_kernel(below_ref, p0, p1, p2, p3, x_ref, out_ref):
    updated = below_ref[...] - ((p0[...] + p1[...]) + (p2[...] + p3[...]))
    out_ref[...] = dot3(split(updated), split(x_ref[...]), NT)


def swap(x, axis, size, step):
    return lax.ppermute(x, axis, [(i, i ^ step) for i in range(size)])


def tree(a, b, c, d):
    return (a + b) + (c + d)


def sum_near(x, rows_n, near_n):
    half = rows_n // 2

    def move(source):
        pairs = []
        for r in range(rows_n):
            z, rest = divmod(r, half)
            for n in range(near_n):
                m, w = source(n, z)
                pairs.append(((w * half + rest) * near_n + m % near_n, r * near_n + n))
        return lax.ppermute(x, ("rows", "near"), pairs)

    far_off = move(lambda n, z: (n + 2, 1 - z))
    next_1 = move(lambda n, z: (n + 2 * z - 1, 1 - z))
    next_2 = move(lambda n, z: (n + 1 - 2 * z, z))
    return (x + far_off) + (next_1 + next_2)


def body(sizes, diag_block, history_rows, panel_below, history_below):
    rows_n, near_n, far_n = sizes
    panel = diag_block.shape[0]
    mine, depth = history_rows.shape
    share = panel_below.shape[0]
    place = lax.axis_index("rows")
    me = place.reshape(1)
    at = jnp.stack([lax.axis_index("near"), lax.axis_index("far")])
    core = lambda x: swap(x, "rows", rows_n, 1)
    along_y = lambda x, k: swap(x, "rows", rows_n, 2 * k)
    other_z = swap(history_rows, "rows", rows_n, 8)
    low = place < rows_n // 2
    pair = jnp.concatenate([jnp.where(low, history_rows, other_z), jnp.where(low, other_z, history_rows)], 0)
    y1, y3 = along_y(pair, 1), along_y(pair, 3)
    close = [pair, y1, y3]
    close_other = [core(x) for x in close]
    schur_part = call(
        schur_kernel,
        jax.ShapeDtypeStruct((2 * mine, panel), F32),
        [SMEM] + [VMEM] * 6,
        [me] + close + close_other,
        scratch=[pltpu.VMEM((panel, depth), BF16)] * 2,
        flops=24 * mine * depth * panel,
        moved=8 * panel * depth,
    )
    schur_part, y1_half, y3_half = lax.optimization_barrier((schur_part, y1[mine:], y3[:mine]))
    y2 = [along_y(y3_half, 1), along_y(y1_half, 3)]
    schur_part = tree(schur_part, *[swap(schur_part, "far", far_n, k) for k in (1, 2, 3)])
    schur_part = sum_near(schur_part, rows_n, near_n)
    schur_pieces = [schur_part] + [along_y(schur_part, k) for k in (1, 2, 3)]
    schur_pieces = schur_pieces + [core(x) for x in schur_pieces]
    gathered = jax.ShapeDtypeStruct((panel, depth), BF16)
    hi, lo = call(
        assemble_kernel,
        (gathered, gathered),
        [SMEM] + [VMEM] * 10,
        [me] + close + y2 + close_other + [core(x) for x in y2],
        moved=8 * panel * depth,
    )
    below = history_below.reshape(near_n, far_n, share, depth)
    parts = [product(at, k, below, hi, lo) for k in (0, 1, 2, 3)]
    parts = [parts[0]] + [swap(parts[k], "far", far_n, k) for k in (1, 2, 3)]
    quarter = lambda p, j: p[j * share:(j + 1) * share]
    sums = [tree(*[quarter(p, j) for p in parts]) for j in range(near_n)]
    sums = [sums[0]] + [swap(sums[j], "near", near_n, j) for j in (1, 2, 3)]
    square = jax.ShapeDtypeStruct((panel, panel), F32)
    diag_factor, inverse = call(
        cholesky_kernel,
        (square, square),
        [SMEM] + [VMEM] * 9,
        [me, diag_block] + schur_pieces,
        scratch=[pltpu.VMEM((panel, panel), F32)],
        flops=2 * panel**3,
        moved=16 * panel * panel,
    )
    panel_factor = call(
        final_kernel,
        jax.ShapeDtypeStruct((share, panel), F32),
        [VMEM] * 6,
        [panel_below] + sums + [inverse],
        flops=6 * share * panel * panel,
        moved=8 * panel * panel,
    )
    return (panel_factor, diag_factor)


def solution(mesh):
    sizes = tuple(mesh.shape[name] for name in ("rows", "near", "far"))
    return jax.shard_map(
        functools.partial(body, sizes),
        mesh=mesh,
        in_specs=(
            P(),
            P("rows", ("near", "far")),
            P(("rows", "near", "far"), None),
            P("rows", ("near", "far")),
        ),
        out_specs=(P(("rows", "near", "far"), None), P()),
        check_vma=False,
    )
```

```python
import functools

import jax
import jax.numpy as jnp
from jax import lax
from jax.experimental import pallas as pl
from jax.experimental.pallas import tpu as pltpu
from jax.sharding import PartitionSpec as P

F32, BF16 = jnp.float32, jnp.bfloat16
NT = (((1,), (1,)), ((), ()))
NN = (((1,), (0,)), ((), ()))
VMEM = pl.BlockSpec(memory_space=pltpu.VMEM)
SMEM = pl.BlockSpec(memory_space=pltpu.SMEM)


def split(x):
    hi = x.astype(BF16)
    return hi, (x - hi.astype(F32)).astype(BF16)


def dot3(a, b, dims):
    d = lambda x, y: lax.dot_general(x, y, dims, preferred_element_type=F32)
    return d(a[0], b[1]) + d(a[1], b[0]) + d(a[0], b[0])


def call(kernel, out_shape, in_specs, args, scratch=(), flops=0, moved=0, vmem=16, aliases=()):
    outs = jax.tree.map(lambda _: VMEM, out_shape)
    return pl.pallas_call(
        kernel,
        out_shape=out_shape,
        in_specs=in_specs,
        out_specs=outs,
        scratch_shapes=list(scratch),
        input_output_aliases=dict(aliases),
        cost_estimate=pl.CostEstimate(flops=flops, bytes_accessed=moved, transcendentals=0),
        compiler_params=pltpu.CompilerParams(vmem_limit_bytes=vmem * 2**20),
    )(*args)


def at_rows(me, z, y_step, core_step, size):
    place = z * 8 + lax.rem(me ^ (y_step * 2 + core_step), 8)
    return pl.ds(pl.multiple_of(place * size, size), size)


def slot_of(shape, size):
    return lax.rem(lax.broadcasted_iota(jnp.int32, shape, 1) // (2 * size), 4)


def schur_kernel(me_ref, *refs):
    pieces, (out_ref, hi_ref, lo_ref) = refs[:6], refs[6:]
    me = me_ref[0]
    size = pieces[0].shape[0] // 2
    for core_step in range(2):
        for i, y_step in enumerate((0, 1, 3)):
            hi, lo = split(pieces[core_step * 3 + i][...])
            for z in range(2):
                part = slice(z * size, (z + 1) * size)
                for slot in (y_step, 2) if y_step == 3 else (y_step,):
                    at = at_rows(me, z, slot, core_step, size)
                    hi_ref[at, :] = hi[part]
                    lo_ref[at, :] = lo[part]
    left = split(jnp.concatenate([pieces[0][...], pieces[1][...]], 0))
    both = dot3(left, (hi_ref[...], lo_ref[...]), NT)
    here, near = both[:2 * size], both[2 * size:]
    y = lax.rem(me // 2, 4)
    out_ref[...] = jnp.where(slot_of(here.shape, size) == (y ^ 2), near, here)


def complete_kernel(me_ref, *refs):
    pieces, (hi_ref, lo_ref) = refs[:4], refs[6:]
    me = me_ref[0]
    size = pieces[0].shape[0]
    for core_step in range(2):
        for z in range(2):
            at = at_rows(me, z, 2, core_step, size)
            hi_ref[at, :], lo_ref[at, :] = split(pieces[core_step * 2 + z][...])


def product_kernel(step, at_ref, below_ref, hi_ref, lo_ref, out_ref):
    near, far = at_ref[0], at_ref[1] ^ step
    rows = jnp.concatenate([below_ref[near ^ j, far] for j in range(below_ref.shape[0])], 0)
    out_ref[...] = dot3(split(rows), (hi_ref[...], lo_ref[...]), NT)


def product(at, step, below, hi, lo):
    near_n, far_n, share, depth = below.shape
    panel = hi.shape[0]
    return call(
        functools.partial(product_kernel, step),
        jax.ShapeDtypeStruct((near_n * share, panel), F32),
        [SMEM] + [VMEM] * 3,
        [at, below, hi, lo],
        flops=11 * near_n * share * depth * panel,
        moved=6 * 2**20,
    )


def recip(x):
    r = pl.reciprocal(x, approx=True)
    return r * (2.0 - x * r)


def factor_block(rows, nb, sc):
    groups = len(rows)
    lane = lax.broadcasted_iota(jnp.int32, (8, nb), 1)
    sub = lax.broadcasted_iota(jnp.int32, (8, nb), 0)
    rows = list(rows)
    inv = [jnp.where(lane == sub + 8 * g, 1.0, 0.0) for g in range(groups)]
    bc = lambda x, k: jnp.broadcast_to(x[k:k + 1, :], (8, nb))
    col = lambda g, t, k: jnp.broadcast_to(rows[g][:, 8 * t + k:8 * t + k + 1], (8, nb))

    def stack(parts):
        out = parts[7]
        for k in range(7):
            out = jnp.where(sub == k, parts[k], out)
        return out

    for t in range(groups):
        own = [col(t, t, k) for k in range(8)]
        p = t % 2
        for m in range(8):
            sc[p, m] = own[m]
        sc[p, 8] = rows[t]
        sc[p, 9] = inv[t]
        lb = lambda m, s: jnp.broadcast_to(sc[p, m, s:s + 1, :], (8, nb))
        e = [[lb(m, s) for m in range(s + 1)] for s in range(8)]
        u = [lb(8, k) for k in range(8)]
        v = [lb(9, k) for k in range(8)]
        diag, pairs = [], []
        for k in range(0, 8, 2):
            a, b, c = e[k][k], e[k + 1][k], e[k + 1][k + 1]
            det = a * c - b * b
            ra, rd = recip(a), recip(det)
            r1 = a * rd
            diag += [a, det * ra]
            low = b * ra
            u[k + 1] = u[k + 1] - low * u[k]
            v[k + 1] = v[k + 1] - low * v[k]
            for s in range(k + 2, 8):
                l0 = e[s][k] * ra
                e[s][k + 1] = e[s][k + 1] - l0 * b
                l1 = e[s][k + 1] * r1
                for m in range(k + 2, s + 1):
                    e[s][m] = (e[s][m] - l0 * e[m][k]) - l1 * e[m][k + 1]
                u[s] = (u[s] - l0 * u[k]) - l1 * u[k + 1]
                v[s] = (v[s] - l0 * v[k]) - l1 * v[k + 1]
            pairs.append((ra, r1))
        for g in range(t + 1, min(t + 1 + 3, groups)):
            f = [col(g, t, k) for k in range(8)]
            for k in range(0, 8, 2):
                ra, r1 = pairs[k // 2]
                f0 = f[k] * ra
                f1 = (f[k + 1] - f0 * e[k + 1][k]) * r1
                for m in range(k + 2, 8):
                    f[m] = (f[m] - f0 * e[m][k]) - f1 * e[m][k + 1]
                rows[g] = (rows[g] - f0 * u[k]) - f1 * u[k + 1]
                inv[g] = (inv[g] - f0 * v[k]) - f1 * v[k + 1]
        scale = lax.rsqrt(stack(diag))
        rows[t] = jnp.where(lane >= sub + 8 * t, stack(u) * scale, 0.0)
        inv[t] = stack(v) * scale
        if t + 1 + 3 < groups:
            both = jnp.concatenate([rows[t], inv[t]], 1)
            hi = both.astype(BF16).astype(F32)
            lo = both - hi
            left = jnp.concatenate([hi[:, :nb], lo[:, :nb], hi[:, :nb], lo[:, :nb]], 0).astype(BF16)
            right = jnp.concatenate([hi, hi, lo, lo], 0).astype(BF16)
            step = lax.dot_general(left, right, (((0,), (0,)), ((), ())), preferred_element_type=F32)
            for g in range(t + 1 + 3, groups):
                rows[g] = rows[g] - step[8 * g:8 * g + 8, :nb]
                inv[g] = inv[g] - step[8 * g:8 * g + 8, nb:]
    return rows, inv


def factor_columns(first, count, w_ref, l_ref, x_ref, sc_ref):
    n = w_ref.shape[0]
    nb = 128
    blk = lambda i: slice(i * nb, (i + 1) * nb)
    for b in range(first, first + count):
        rows = [w_ref[b * nb + 8 * g:b * nb + 8 * g + 8, blk(b)] for g in range(nb // 8)]
        up, inv = factor_block(rows, nb, sc_ref)
        x11 = jnp.concatenate(inv, 0)
        l_ref[blk(b), blk(b)] = jnp.concatenate(up, 0).T
        x_ref[blk(b), blk(b)] = x11
        if (b + 1) * nb < n:
            rest = slice((b + 1) * nb, n)
            l21 = dot3(split(w_ref[rest, blk(b)]), split(x11), NT)
            l_ref[rest, blk(b)] = l21
            ls = split(l21)
            w_ref[rest, rest] = w_ref[rest, rest] - dot3(ls, ls, NT)
        if b > 0:
            done = slice(0, b * nb)
            t = dot3(split(l_ref[blk(b), done]), split(x_ref[done, done]), NN)
            x_ref[blk(b), done] = -dot3(split(x11), split(t), NN)


def leading_kernel(me_ref, diag_ref, *refs):
    pieces, (w_ref, l_ref, x_ref, sc_ref) = refs[:8], refs[8:]
    me = me_ref[0]
    size = pieces[0].shape[0] // 2
    y = lax.rem(me // 2, 4)
    for core_step in range(2):
        for y_step in range(4):
            own = pieces[core_step * 4 + y_step][...]
            other = pieces[core_step * 4 + (y_step ^ 1)][...]
            tiles = [other[:, i:i + 128] for i in range(0, other.shape[1], 128)]
            other = jnp.concatenate([pltpu.roll(t, 64, 1) for t in tiles], 1)
            whole = jnp.where(slot_of(own.shape, size) == (y ^ y_step ^ 2), other, own)
            for z in range(2):
                at = at_rows(me, z, y_step, core_step, size)
                w_ref[at, :] = diag_ref[at, :] - whole[z * size:(z + 1) * size]
    l_ref[...] = jnp.zeros_like(l_ref)
    x_ref[...] = jnp.zeros_like(x_ref)
    factor_columns(0, w_ref.shape[0] // 128 - 1, w_ref, l_ref, x_ref, sc_ref)


def last_kernel(w_in, l_in, x_in, l_ref, x_ref, w_ref, sc_ref):
    w_ref[...] = w_in[...]
    l_ref[...] = l_in[...]
    x_ref[...] = x_in[...]
    factor_columns(w_ref.shape[0] // 128 - 1, 1, w_ref, l_ref, x_ref, sc_ref)


def final_kernel(below_ref, p0, p1, p2, p3, x_ref, out_ref):
    updated = below_ref[...] - ((p0[...] + p1[...]) + (p2[...] + p3[...]))
    out_ref[...] = dot3(split(updated), split(x_ref[...]), NT)


def swap(x, axis, size, step):
    return lax.ppermute(x, axis, [(i, i ^ step) for i in range(size)])


def tree(a, b, c, d):
    return (a + b) + (c + d)


def sum_near(x, rows_n, near_n):
    half = rows_n // 2

    def move(source):
        pairs = []
        for r in range(rows_n):
            z, rest = divmod(r, half)
            for n in range(near_n):
                m, w = source(n, z)
                pairs.append(((w * half + rest) * near_n + m % near_n, r * near_n + n))
        return lax.ppermute(x, ("rows", "near"), pairs)

    far_off = move(lambda n, z: (n + 2, 1 - z))
    next_1 = move(lambda n, z: (n + 2 * z - 1, 1 - z))
    next_2 = move(lambda n, z: (n + 1 - 2 * z, z))
    return (x + far_off) + (next_1 + next_2)


def body(sizes, diag_block, history_rows, panel_below, history_below):
    rows_n, near_n, far_n = sizes
    panel = diag_block.shape[0]
    mine, depth = history_rows.shape
    share = panel_below.shape[0]
    place = lax.axis_index("rows")
    me = place.reshape(1)
    at = jnp.stack([lax.axis_index("near"), lax.axis_index("far")])
    core = lambda x: swap(x, "rows", rows_n, 1)
    along_y = lambda x, k: swap(x, "rows", rows_n, 2 * k)
    other_z = swap(history_rows, "rows", rows_n, 8)
    low = place < rows_n // 2
    pair = jnp.concatenate([jnp.where(low, history_rows, other_z), jnp.where(low, other_z, history_rows)], 0)
    y1, y3 = along_y(pair, 1), along_y(pair, 3)
    close = [pair, y1, y3]
    close_other = [core(x) for x in close]
    gathered = jax.ShapeDtypeStruct((panel, depth), BF16)
    schur_part, hi, lo = call(
        schur_kernel,
        (jax.ShapeDtypeStruct((2 * mine, panel), F32), gathered, gathered),
        [SMEM] + [VMEM] * 6,
        [me] + close + close_other,
        flops=24 * mine * depth * panel,
        moved=8 * panel * depth,
    )
    y2 = [along_y(y3[:mine], 1), along_y(y1[mine:], 3)]
    *y2_late, _ = lax.optimization_barrier((*y2, schur_part))
    by_far = [swap(schur_part, "far", far_n, k) for k in (1, 2, 3)]
    hi, lo = call(
        complete_kernel,
        (gathered, gathered),
        [SMEM] + [VMEM] * 6,
        [me] + y2_late + [core(x) for x in y2_late] + [hi, lo],
        moved=2 * panel * depth,
        aliases=((5, 0), (6, 1)),
    )
    below = history_below.reshape(near_n, far_n, share, depth)
    parts = [product(at, k, below, hi, lo) for k in (0, 1, 2, 3)]
    schur_part = tree(schur_part, *by_far)
    schur_part = sum_near(schur_part, rows_n, near_n)
    schur_pieces = [schur_part] + [along_y(schur_part, k) for k in (1, 2, 3)]
    schur_pieces = schur_pieces + [core(x) for x in schur_pieces]
    parts = [parts[0]] + [swap(parts[k], "far", far_n, k) for k in (1, 2, 3)]
    quarter = lambda p, j: p[j * share:(j + 1) * share]
    sums = [tree(*[quarter(p, j) for p in parts]) for j in range(near_n)]
    square = jax.ShapeDtypeStruct((panel, panel), F32)
    broadcasts = pltpu.VMEM((2, 10, 8, 128), F32)
    leading = call(
        leading_kernel,
        (square,) * 3,
        [SMEM] + [VMEM] * 9,
        [me, diag_block] + schur_pieces,
        scratch=[broadcasts],
        flops=96 * panel**3,
        moved=16 * panel * panel,
    )
    *leading, sums[1], sums[2], sums[3] = lax.optimization_barrier((*leading, *sums[1:]))
    sums = [sums[0]] + [swap(sums[j], "near", near_n, j) for j in (1, 2, 3)]
    diag_factor, inverse = call(
        last_kernel,
        (square,) * 2,
        [VMEM] * 3,
        leading,
        scratch=[pltpu.VMEM((panel, panel), F32), broadcasts],
        flops=24 * panel**3,
        moved=16 * panel * panel,
    )
    panel_factor = call(
        final_kernel,
        jax.ShapeDtypeStruct((share, panel), F32),
        [VMEM] * 6,
        [panel_below] + sums + [inverse],
        flops=6 * share * panel * panel,
        moved=8 * panel * panel,
    )
    return (panel_factor, diag_factor)


def solution(mesh):
    sizes = tuple(mesh.shape[name] for name in ("rows", "near", "far"))
    return jax.shard_map(
        functools.partial(body, sizes),
        mesh=mesh,
        in_specs=(
            P(),
            P("rows", ("near", "far")),
            P(("rows", "near", "far"), None),
            P("rows", ("near", "far")),
        ),
        out_specs=(P(("rows", "near", "far"), None), P()),
        check_vma=False,
    )
```

```python
import functools

import jax
import jax.numpy as jnp
from jax import lax
from jax.experimental import pallas as pl
from jax.experimental.pallas import tpu as pltpu
from jax.sharding import PartitionSpec as P

F32, BF16 = jnp.float32, jnp.bfloat16
NT = (((1,), (1,)), ((), ()))
NN = (((1,), (0,)), ((), ()))
VMEM = pl.BlockSpec(memory_space=pltpu.VMEM)
SMEM = pl.BlockSpec(memory_space=pltpu.SMEM)
PRODUCT_VMEM = 45


def split(x):
    hi = x.astype(BF16)
    return hi, (x - hi.astype(F32)).astype(BF16)


def dot3(a, b, dims):
    d = lambda x, y: lax.dot_general(x, y, dims, preferred_element_type=F32)
    return d(a[0], b[1]) + d(a[1], b[0]) + d(a[0], b[0])


def call(kernel, out_shape, in_specs, args, scratch=(), flops=0, moved=0, vmem=16, aliases=()):
    outs = jax.tree.map(lambda _: VMEM, out_shape)
    return pl.pallas_call(
        kernel,
        out_shape=out_shape,
        in_specs=in_specs,
        out_specs=outs,
        scratch_shapes=list(scratch),
        input_output_aliases=dict(aliases),
        cost_estimate=pl.CostEstimate(flops=flops, bytes_accessed=moved, transcendentals=0),
        compiler_params=pltpu.CompilerParams(vmem_limit_bytes=vmem * 2**20),
    )(*args)


def at_rows(me, z, y_step, core_step, size):
    place = z * 8 + lax.rem(me ^ (y_step * 2 + core_step), 8)
    return pl.ds(pl.multiple_of(place * size, size), size)


def slot_of(shape, size):
    return lax.rem(lax.broadcasted_iota(jnp.int32, shape, 1) // (2 * size), 4)


def schur_kernel(me_ref, *refs):
    pieces, (out_ref, hi_ref, lo_ref) = refs[:6], refs[6:]
    me = me_ref[0]
    size = pieces[0].shape[0] // 2
    for core_step in range(2):
        for i, y_step in enumerate((0, 1, 3)):
            hi, lo = split(pieces[core_step * 3 + i][...])
            for z in range(2):
                part = slice(z * size, (z + 1) * size)
                for slot in (y_step, 2) if y_step == 3 else (y_step,):
                    at = at_rows(me, z, slot, core_step, size)
                    hi_ref[at, :] = hi[part]
                    lo_ref[at, :] = lo[part]
    left = split(jnp.concatenate([pieces[0][...], pieces[1][...]], 0))
    both = dot3(left, (hi_ref[...], lo_ref[...]), NT)
    here, near = both[:2 * size], both[2 * size:]
    y = lax.rem(me // 2, 4)
    out_ref[...] = jnp.where(slot_of(here.shape, size) == (y ^ 2), near, here)


def complete_kernel(me_ref, p0, p1, q0, q1, _, __, hi_ref, lo_ref):
    me = me_ref[0]
    size = p0.shape[0] // 2
    first = lax.rem(me, 2) == 0
    for core_step, (even, odd) in enumerate(((p0, p1), (q1, q0))):
        for z in range(2):
            part = slice(z * size, (z + 1) * size)
            at = at_rows(me, z, 2, core_step, size)
            hi_ref[at, :], lo_ref[at, :] = split(jnp.where(first, even[part, :], odd[part, :]))


def long_dot(rows, hi, lo):
    left_hi, left_lo = split(rows)
    left = jnp.concatenate([left_hi, left_lo, left_hi], 1)
    right = jnp.concatenate([lo, hi, hi], 1)
    return lax.dot_general(left, right, NT, preferred_element_type=F32)


def product_kernel(at_ref, below_ref, hi_ref, lo_ref, a_send, b_send, a_keep, b_keep, held, sems):
    near, far = at_ref[0], at_ref[1]
    near_n, _, share, _ = below_ref.shape
    half = a_send.shape[2]
    groups = ((1, 2), (3, 0))
    copies = {}
    for k in (1, 2, 3, 0):
        for j in range(near_n):
            to = held.at[k, pl.ds(j * share, share)]
            copies[k, j] = pltpu.make_async_copy(below_ref.at[near ^ j, far ^ k], to, sems.at[k, j])
            copies[k, j].start()
    places = {1: ((a_send, 0), (b_keep, 1)), 2: ((a_send, 1), (b_send, 1)),
              3: ((a_keep, 1), (b_send, 0)), 0: ((a_keep, 0), (b_keep, 0))}
    for group in groups:
        for k in group:
            for j in range(near_n):
                copies[k, j].wait()
        out = long_dot(jnp.concatenate([held[k] for k in group], 0), hi_ref[...], lo_ref[...])
        size = out.shape[0] // 2
        for i, k in enumerate(group):
            (a, at_a), (b, at_b) = places[k]
            a[at_a] = out[i * size:(i + 1) * size, :half]
            b[at_b] = out[i * size:(i + 1) * size, half:]


def products(at, below, hi, lo):
    near_n, far_n, share, depth = below.shape
    panel = hi.shape[0]
    rows = near_n * share
    return call(
        product_kernel,
        (jax.ShapeDtypeStruct((2, rows, panel // 2), F32),) * 4,
        [SMEM, pl.BlockSpec(memory_space=pl.ANY), VMEM, VMEM],
        [at, below, hi, lo],
        scratch=[pltpu.VMEM((far_n, rows, depth), F32), pltpu.SemaphoreType.DMA((far_n, near_n))],
        flops=9 * far_n * rows * depth * panel,
        moved=6 * 2**20,
        vmem=PRODUCT_VMEM,
    )


def middle_kernel(a_keep, a_got, b_keep, b_got, a_out, b_out):
    a_out[...] = a_keep[1] + a_got[1]
    b_out[...] = b_keep[1] + b_got[1]


def combine_kernel(a_keep, a_got, a_last, b_keep, b_got, b_last, *outs):
    share, panel = outs[0].shape
    for j, out in enumerate(outs):
        rows = slice(j * share, (j + 1) * share)
        out[:, :panel // 2] = a_keep[0, rows] + a_got[0, rows] + a_last[rows]
        out[:, panel // 2:] = b_keep[0, rows] + b_got[0, rows] + b_last[rows]


def recip(x):
    r = pl.reciprocal(x, approx=True)
    return r * (2.0 - x * r)


def factor_block(rows, nb, sc):
    groups = len(rows)
    lane = lax.broadcasted_iota(jnp.int32, (8, nb), 1)
    sub = lax.broadcasted_iota(jnp.int32, (8, nb), 0)
    rows = list(rows)
    inv = [jnp.where(lane == sub + 8 * g, 1.0, 0.0) for g in range(groups)]
    bc = lambda x, k: jnp.broadcast_to(x[k:k + 1, :], (8, nb))
    col = lambda g, t, k: jnp.broadcast_to(rows[g][:, 8 * t + k:8 * t + k + 1], (8, nb))

    def stack(parts):
        out = parts[7]
        for k in range(7):
            out = jnp.where(sub == k, parts[k], out)
        return out

    for t in range(groups):
        own = [col(t, t, k) for k in range(8)]
        p = t % 2
        for m in range(8):
            sc[p, m] = own[m]
        sc[p, 8] = rows[t]
        sc[p, 9] = inv[t]
        lb = lambda m, s: jnp.broadcast_to(sc[p, m, s:s + 1, :], (8, nb))
        e = [[lb(m, s) for m in range(s + 1)] for s in range(8)]
        u = [lb(8, k) for k in range(8)]
        v = [lb(9, k) for k in range(8)]
        diag, pairs = [], []
        for k in range(0, 8, 2):
            a, b, c = e[k][k], e[k + 1][k], e[k + 1][k + 1]
            det = a * c - b * b
            ra, rd = recip(a), recip(det)
            r1 = a * rd
            diag += [a, det * ra]
            low = b * ra
            u[k + 1] = u[k + 1] - low * u[k]
            v[k + 1] = v[k + 1] - low * v[k]
            for s in range(k + 2, 8):
                l0 = e[s][k] * ra
                e[s][k + 1] = e[s][k + 1] - l0 * b
                l1 = e[s][k + 1] * r1
                for m in range(k + 2, s + 1):
                    e[s][m] = (e[s][m] - l0 * e[m][k]) - l1 * e[m][k + 1]
                u[s] = (u[s] - l0 * u[k]) - l1 * u[k + 1]
                v[s] = (v[s] - l0 * v[k]) - l1 * v[k + 1]
            pairs.append((ra, r1))
        for g in range(t + 1, min(t + 1 + 3, groups)):
            f = [col(g, t, k) for k in range(8)]
            for k in range(0, 8, 2):
                ra, r1 = pairs[k // 2]
                f0 = f[k] * ra
                f1 = (f[k + 1] - f0 * e[k + 1][k]) * r1
                for m in range(k + 2, 8):
                    f[m] = (f[m] - f0 * e[m][k]) - f1 * e[m][k + 1]
                rows[g] = (rows[g] - f0 * u[k]) - f1 * u[k + 1]
                inv[g] = (inv[g] - f0 * v[k]) - f1 * v[k + 1]
        scale = lax.rsqrt(stack(diag))
        rows[t] = jnp.where(lane >= sub + 8 * t, stack(u) * scale, 0.0)
        inv[t] = stack(v) * scale
        if t + 1 + 3 < groups:
            both = jnp.concatenate([rows[t], inv[t]], 1)
            hi = both.astype(BF16).astype(F32)
            lo = both - hi
            left = jnp.concatenate([hi[:, :nb], lo[:, :nb], hi[:, :nb], lo[:, :nb]], 0).astype(BF16)
            right = jnp.concatenate([hi, hi, lo, lo], 0).astype(BF16)
            step = lax.dot_general(left, right, (((0,), (0,)), ((), ())), preferred_element_type=F32)
            for g in range(t + 1 + 3, groups):
                rows[g] = rows[g] - step[8 * g:8 * g + 8, :nb]
                inv[g] = inv[g] - step[8 * g:8 * g + 8, nb:]
    return rows, inv


def factor_columns(w_ref, l_ref, x_ref, sc_ref):
    n = w_ref.shape[0]
    nb = 128
    blk = lambda i: slice(i * nb, (i + 1) * nb)
    for b in range(n // nb):
        rows = [w_ref[b * nb + 8 * g:b * nb + 8 * g + 8, blk(b)] for g in range(nb // 8)]
        up, inv = factor_block(rows, nb, sc_ref)
        x11 = jnp.concatenate(inv, 0)
        l_ref[blk(b), blk(b)] = jnp.concatenate(up, 0).T
        x_ref[blk(b), blk(b)] = x11
        if (b + 1) * nb < n:
            rest = slice((b + 1) * nb, n)
            l21 = dot3(split(w_ref[rest, blk(b)]), split(x11), NT)
            l_ref[rest, blk(b)] = l21
            ls = split(l21)
            w_ref[rest, rest] = w_ref[rest, rest] - dot3(ls, ls, NT)
        if b > 0:
            done = slice(0, b * nb)
            t = dot3(split(l_ref[blk(b), done]), split(x_ref[done, done]), NN)
            x_ref[blk(b), done] = -dot3(split(x11), split(t), NN)


def cholesky_kernel(me_ref, diag_ref, *refs):
    pieces, (l_ref, x_ref, w_ref, sc_ref) = refs[:8], refs[8:]
    me = me_ref[0]
    size = pieces[0].shape[0] // 2
    y = lax.rem(me // 2, 4)
    for core_step in range(2):
        for y_step in range(4):
            own = pieces[core_step * 4 + y_step][...]
            other = pieces[core_step * 4 + (y_step ^ 1)][...]
            tiles = [other[:, i:i + 128] for i in range(0, other.shape[1], 128)]
            other = jnp.concatenate([pltpu.roll(t, 64, 1) for t in tiles], 1)
            whole = jnp.where(slot_of(own.shape, size) == (y ^ y_step ^ 2), other, own)
            for z in range(2):
                at = at_rows(me, z, y_step, core_step, size)
                w_ref[at, :] = diag_ref[at, :] - whole[z * size:(z + 1) * size]
    l_ref[...] = jnp.zeros_like(l_ref)
    x_ref[...] = jnp.zeros_like(x_ref)
    factor_columns(w_ref, l_ref, x_ref, sc_ref)


def final_kernel(below_ref, p0, p1, p2, p3, x_ref, out_ref):
    updated = below_ref[...] - ((p0[...] + p1[...]) + (p2[...] + p3[...]))
    out_ref[...] = dot3(split(updated), split(x_ref[...]), NT)


def swap(x, axis, size, step):
    return lax.ppermute(x, axis, [(i, i ^ step) for i in range(size)])


def tree(a, b, c, d):
    return (a + b) + (c + d)


def sum_near(x, rows_n, near_n):
    half = rows_n // 2

    def move(source):
        pairs = []
        for r in range(rows_n):
            z, rest = divmod(r, half)
            for n in range(near_n):
                m, w = source(n, z)
                pairs.append(((w * half + rest) * near_n + m % near_n, r * near_n + n))
        return lax.ppermute(x, ("rows", "near"), pairs)

    far_off = move(lambda n, z: (n + 2, 1 - z))
    next_1 = move(lambda n, z: (n + 2 * z - 1, 1 - z))
    next_2 = move(lambda n, z: (n + 1 - 2 * z, z))
    return (x + far_off) + (next_1 + next_2)


def body(sizes, diag_block, history_rows, panel_below, history_below):
    rows_n, near_n, far_n = sizes
    panel = diag_block.shape[0]
    mine, depth = history_rows.shape
    share = panel_below.shape[0]
    place = lax.axis_index("rows")
    me = place.reshape(1)
    at = jnp.stack([lax.axis_index("near"), lax.axis_index("far")])
    core = lambda x: swap(x, "rows", rows_n, 1)
    along_y = lambda x, k: swap(x, "rows", rows_n, 2 * k)
    other_z = swap(history_rows, "rows", rows_n, 8)
    low = place < rows_n // 2
    pair = jnp.concatenate([jnp.where(low, history_rows, other_z), jnp.where(low, other_z, history_rows)], 0)
    y1, y3 = along_y(pair, 1), along_y(pair, 3)
    close = [pair, y1, y3]
    close_other = [core(x) for x in close]
    gathered = jax.ShapeDtypeStruct((panel, depth), BF16)
    schur_part, hi, lo = call(
        schur_kernel,
        (jax.ShapeDtypeStruct((2 * mine, panel), F32), gathered, gathered),
        [SMEM] + [VMEM] * 6,
        [me] + close + close_other,
        flops=24 * mine * depth * panel,
        moved=8 * panel * depth,
    )
    def some(x, core_at, step):
        pairs = [(i, i ^ step) for i in range(rows_n) if i % 2 == core_at]
        return lax.ppermute(x, "rows", pairs)

    y2 = [some(y3, 0, 2), some(y1, 1, 6)]
    *y2_late, _ = lax.optimization_barrier((*y2, schur_part))
    by_far = [swap(schur_part, "far", far_n, k) for k in (1, 2, 3)]
    hi, lo = call(
        complete_kernel,
        (gathered, gathered),
        [SMEM] + [VMEM] * 6,
        [me] + y2_late + [some(y2_late[0], 0, 1), some(y2_late[1], 1, 1), hi, lo],
        moved=2 * panel * depth,
        aliases=((5, 0), (6, 1)),
    )
    below = history_below.reshape(near_n, far_n, share, depth)
    a_send, b_send, a_keep, b_keep = products(at, below, hi, lo)
    *by_far, a_send, b_send = lax.optimization_barrier((*by_far, a_send, b_send))
    schur_part = tree(schur_part, *by_far)
    schur_part = sum_near(schur_part, rows_n, near_n)
    schur_pieces = [schur_part] + [along_y(schur_part, k) for k in (1, 2, 3)]
    schur_pieces = schur_pieces + [core(x) for x in schur_pieces]
    a_got, b_got = swap(a_send, "far", far_n, 1), swap(b_send, "far", far_n, 3)
    a_got, b_got, _ = lax.optimization_barrier((a_got, b_got, schur_part))
    block = jax.ShapeDtypeStruct(a_send.shape[1:], F32)
    a_next, b_next = call(middle_kernel, (block, block), [VMEM] * 4, [a_keep, a_got, b_keep, b_got], moved=2**20)
    a_last, b_last = swap(a_next, "far", far_n, 3), swap(b_next, "far", far_n, 1)
    sums = call(
        combine_kernel,
        (jax.ShapeDtypeStruct((share, panel), F32),) * near_n,
        [VMEM] * 6,
        [a_keep, a_got, a_last, b_keep, b_got, b_last],
        moved=2**20,
    )
    sums = [sums[0]] + [swap(sums[j], "near", near_n, j) for j in (1, 2, 3)]
    square = jax.ShapeDtypeStruct((panel, panel), F32)
    diag_factor, inverse = call(
        cholesky_kernel,
        (square,) * 2,
        [SMEM] + [VMEM] * 9,
        [me, diag_block] + schur_pieces,
        scratch=[pltpu.VMEM((panel, panel), F32), pltpu.VMEM((2, 10, 8, 128), F32)],
        flops=120 * panel**3,
        moved=16 * panel * panel,
    )
    panel_factor = call(
        final_kernel,
        jax.ShapeDtypeStruct((share, panel), F32),
        [VMEM] * 6,
        [panel_below] + sums + [inverse],
        flops=6 * share * panel * panel,
        moved=8 * panel * panel,
    )
    return (panel_factor, diag_factor)


def solution(mesh):
    sizes = tuple(mesh.shape[name] for name in ("rows", "near", "far"))
    return jax.shard_map(
        functools.partial(body, sizes),
        mesh=mesh,
        in_specs=(
            P(),
            P("rows", ("near", "far")),
            P(("rows", "near", "far"), None),
            P("rows", ("near", "far")),
        ),
        out_specs=(P(("rows", "near", "far"), None), P()),
        check_vma=False,
    )
```

```python
import functools

import jax
import jax.numpy as jnp
from jax import lax
from jax.experimental import pallas as pl
from jax.experimental.pallas import tpu as pltpu
from jax.sharding import PartitionSpec as P

F32, BF16 = jnp.float32, jnp.bfloat16
NT = (((1,), (1,)), ((), ()))
NN = (((1,), (0,)), ((), ()))
VMEM = pl.BlockSpec(memory_space=pltpu.VMEM)
SMEM = pl.BlockSpec(memory_space=pltpu.SMEM)
PRODUCT_VMEM = 45


def split(x):
    hi = x.astype(BF16)
    return hi, (x - hi.astype(F32)).astype(BF16)


def dot3(a, b, dims):
    d = lambda x, y: lax.dot_general(x, y, dims, preferred_element_type=F32)
    return d(a[0], b[1]) + d(a[1], b[0]) + d(a[0], b[0])


def call(kernel, out_shape, in_specs, args, scratch=(), flops=0, moved=0, vmem=16, aliases=()):
    outs = jax.tree.map(lambda _: VMEM, out_shape)
    return pl.pallas_call(
        kernel,
        out_shape=out_shape,
        in_specs=in_specs,
        out_specs=outs,
        scratch_shapes=list(scratch),
        input_output_aliases=dict(aliases),
        cost_estimate=pl.CostEstimate(flops=flops, bytes_accessed=moved, transcendentals=0),
        compiler_params=pltpu.CompilerParams(vmem_limit_bytes=vmem * 2**20),
    )(*args)


def at_rows(me, z, y_step, core_step, size):
    place = z * 8 + lax.rem(me ^ (y_step * 2 + core_step), 8)
    return pl.ds(pl.multiple_of(place * size, size), size)


def slot_of(shape, size):
    return lax.rem(lax.broadcasted_iota(jnp.int32, shape, 1) // (2 * size), 4)


def schur_kernel(me_ref, *refs):
    pieces, (out_ref, hi_ref, lo_ref) = refs[:6], refs[6:]
    me = me_ref[0]
    size = pieces[0].shape[0] // 2
    for core_step in range(2):
        for i, y_step in enumerate((0, 1, 3)):
            hi, lo = split(pieces[core_step * 3 + i][...])
            for z in range(2):
                part = slice(z * size, (z + 1) * size)
                for slot in (y_step, 2) if y_step == 3 else (y_step,):
                    at = at_rows(me, z, slot, core_step, size)
                    hi_ref[at, :] = hi[part]
                    lo_ref[at, :] = lo[part]
    left = split(jnp.concatenate([pieces[0][...], pieces[1][...]], 0))
    both = dot3(left, (hi_ref[...], lo_ref[...]), NT)
    here, near = both[:2 * size], both[2 * size:]
    y = lax.rem(me // 2, 4)
    out_ref[...] = jnp.where(slot_of(here.shape, size) == (y ^ 2), near, here)


def complete_kernel(me_ref, *refs):
    pieces, (hi_ref, lo_ref) = refs[:4], refs[6:]
    me = me_ref[0]
    size = pieces[0].shape[0]
    for core_step in range(2):
        for z in range(2):
            at = at_rows(me, z, 2, core_step, size)
            hi_ref[at, :], lo_ref[at, :] = split(pieces[core_step * 2 + z][...])


def long_dot(rows, hi, lo):
    left_hi, left_lo = split(rows)
    left = jnp.concatenate([left_hi, left_lo, left_hi], 1)
    right = jnp.concatenate([lo, hi, hi], 1)
    return lax.dot_general(left, right, NT, preferred_element_type=F32)


def product_kernel(at_ref, below_ref, hi_ref, lo_ref, a_send, b_send, a_keep, b_keep, held, sems):
    near, far = at_ref[0], at_ref[1]
    near_n, _, share, _ = below_ref.shape
    half = a_send.shape[2]
    groups = ((1, 2), (3, 0))
    copies = {}
    for k in (1, 2, 3, 0):
        for j in range(near_n):
            to = held.at[k, pl.ds(j * share, share)]
            copies[k, j] = pltpu.make_async_copy(below_ref.at[near ^ j, far ^ k], to, sems.at[k, j])
            copies[k, j].start()
    places = {1: ((a_send, 0), (b_keep, 1)), 2: ((a_send, 1), (b_send, 1)),
              3: ((a_keep, 1), (b_send, 0)), 0: ((a_keep, 0), (b_keep, 0))}
    for group in groups:
        for k in group:
            for j in range(near_n):
                copies[k, j].wait()
        out = long_dot(jnp.concatenate([held[k] for k in group], 0), hi_ref[...], lo_ref[...])
        size = out.shape[0] // 2
        for i, k in enumerate(group):
            (a, at_a), (b, at_b) = places[k]
            a[at_a] = out[i * size:(i + 1) * size, :half]
            b[at_b] = out[i * size:(i + 1) * size, half:]


def products(at, below, hi, lo):
    near_n, far_n, share, depth = below.shape
    panel = hi.shape[0]
    rows = near_n * share
    return call(
        product_kernel,
        (jax.ShapeDtypeStruct((2, rows, panel // 2), F32),) * 4,
        [SMEM, pl.BlockSpec(memory_space=pl.ANY), VMEM, VMEM],
        [at, below, hi, lo],
        scratch=[pltpu.VMEM((far_n, rows, depth), F32), pltpu.SemaphoreType.DMA((far_n, near_n))],
        flops=9 * far_n * rows * depth * panel,
        moved=6 * 2**20,
        vmem=PRODUCT_VMEM,
    )


def middle_kernel(a_keep, a_got, b_keep, b_got, a_out, b_out):
    a_out[...] = a_keep[1] + a_got[1]
    b_out[...] = b_keep[1] + b_got[1]


def combine_kernel(a_keep, a_got, a_last, b_keep, b_got, b_last, *outs):
    share, panel = outs[0].shape
    for j, out in enumerate(outs):
        rows = slice(j * share, (j + 1) * share)
        out[:, :panel // 2] = a_keep[0, rows] + a_got[0, rows] + a_last[rows]
        out[:, panel // 2:] = b_keep[0, rows] + b_got[0, rows] + b_last[rows]


def recip(x):
    r = pl.reciprocal(x, approx=True)
    return r * (2.0 - x * r)


def factor_block(rows, nb, sc):
    groups = len(rows)
    lane = lax.broadcasted_iota(jnp.int32, (8, nb), 1)
    sub = lax.broadcasted_iota(jnp.int32, (8, nb), 0)
    rows = list(rows)
    inv = [jnp.where(lane == sub + 8 * g, 1.0, 0.0) for g in range(groups)]
    bc = lambda x, k: jnp.broadcast_to(x[k:k + 1, :], (8, nb))
    col = lambda g, t, k: jnp.broadcast_to(rows[g][:, 8 * t + k:8 * t + k + 1], (8, nb))

    def stack(parts):
        out = parts[7]
        for k in range(7):
            out = jnp.where(sub == k, parts[k], out)
        return out

    for t in range(groups):
        own = [col(t, t, k) for k in range(8)]
        p = t % 2
        for m in range(8):
            sc[p, m] = own[m]
        sc[p, 8] = rows[t]
        sc[p, 9] = inv[t]
        lb = lambda m, s: jnp.broadcast_to(sc[p, m, s:s + 1, :], (8, nb))
        e = [[lb(m, s) for m in range(s + 1)] for s in range(8)]
        u = [lb(8, k) for k in range(8)]
        v = [lb(9, k) for k in range(8)]
        diag, pairs = [], []
        for k in range(0, 8, 2):
            a, b, c = e[k][k], e[k + 1][k], e[k + 1][k + 1]
            det = a * c - b * b
            ra, rd = recip(a), recip(det)
            r1 = a * rd
            diag += [a, det * ra]
            low = b * ra
            u[k + 1] = u[k + 1] - low * u[k]
            v[k + 1] = v[k + 1] - low * v[k]
            for s in range(k + 2, 8):
                l0 = e[s][k] * ra
                e[s][k + 1] = e[s][k + 1] - l0 * b
                l1 = e[s][k + 1] * r1
                for m in range(k + 2, s + 1):
                    e[s][m] = (e[s][m] - l0 * e[m][k]) - l1 * e[m][k + 1]
                u[s] = (u[s] - l0 * u[k]) - l1 * u[k + 1]
                v[s] = (v[s] - l0 * v[k]) - l1 * v[k + 1]
            pairs.append((ra, r1))
        for g in range(t + 1, min(t + 1 + 3, groups)):
            f = [col(g, t, k) for k in range(8)]
            for k in range(0, 8, 2):
                ra, r1 = pairs[k // 2]
                f0 = f[k] * ra
                f1 = (f[k + 1] - f0 * e[k + 1][k]) * r1
                for m in range(k + 2, 8):
                    f[m] = (f[m] - f0 * e[m][k]) - f1 * e[m][k + 1]
                rows[g] = (rows[g] - f0 * u[k]) - f1 * u[k + 1]
                inv[g] = (inv[g] - f0 * v[k]) - f1 * v[k + 1]
        scale = lax.rsqrt(stack(diag))
        rows[t] = jnp.where(lane >= sub + 8 * t, stack(u) * scale, 0.0)
        inv[t] = stack(v) * scale
        if t + 1 + 3 < groups:
            both = jnp.concatenate([rows[t], inv[t]], 1)
            hi = both.astype(BF16).astype(F32)
            lo = both - hi
            left = jnp.concatenate([hi[:, :nb], lo[:, :nb], hi[:, :nb], lo[:, :nb]], 0).astype(BF16)
            right = jnp.concatenate([hi, hi, lo, lo], 0).astype(BF16)
            step = lax.dot_general(left, right, (((0,), (0,)), ((), ())), preferred_element_type=F32)
            for g in range(t + 1 + 3, groups):
                rows[g] = rows[g] - step[8 * g:8 * g + 8, :nb]
                inv[g] = inv[g] - step[8 * g:8 * g + 8, nb:]
    return rows, inv


def factor_columns(w_ref, l_ref, x_ref, sc_ref):
    n = w_ref.shape[0]
    nb = 128
    blk = lambda i: slice(i * nb, (i + 1) * nb)
    for b in range(n // nb):
        rows = [w_ref[b * nb + 8 * g:b * nb + 8 * g + 8, blk(b)] for g in range(nb // 8)]
        up, inv = factor_block(rows, nb, sc_ref)
        x11 = jnp.concatenate(inv, 0)
        l_ref[blk(b), blk(b)] = jnp.concatenate(up, 0).T
        x_ref[blk(b), blk(b)] = x11
        if (b + 1) * nb < n:
            rest = slice((b + 1) * nb, n)
            l21 = dot3(split(w_ref[rest, blk(b)]), split(x11), NT)
            l_ref[rest, blk(b)] = l21
            ls = split(l21)
            w_ref[rest, rest] = w_ref[rest, rest] - dot3(ls, ls, NT)
        if b > 0:
            done = slice(0, b * nb)
            t = dot3(split(l_ref[blk(b), done]), split(x_ref[done, done]), NN)
            x_ref[blk(b), done] = -dot3(split(x11), split(t), NN)


def cholesky_kernel(me_ref, diag_ref, *refs):
    pieces, (l_ref, x_ref, w_ref, sc_ref) = refs[:8], refs[8:]
    me = me_ref[0]
    size = pieces[0].shape[0] // 2
    y = lax.rem(me // 2, 4)
    for core_step in range(2):
        for y_step in range(4):
            own = pieces[core_step * 4 + y_step][...]
            other = pieces[core_step * 4 + (y_step ^ 1)][...]
            tiles = [other[:, i:i + 128] for i in range(0, other.shape[1], 128)]
            other = jnp.concatenate([pltpu.roll(t, 64, 1) for t in tiles], 1)
            whole = jnp.where(slot_of(own.shape, size) == (y ^ y_step ^ 2), other, own)
            for z in range(2):
                at = at_rows(me, z, y_step, core_step, size)
                w_ref[at, :] = diag_ref[at, :] - whole[z * size:(z + 1) * size]
    l_ref[...] = jnp.zeros_like(l_ref)
    x_ref[...] = jnp.zeros_like(x_ref)
    factor_columns(w_ref, l_ref, x_ref, sc_ref)


def final_kernel(below_ref, p0, p1, p2, p3, x_ref, out_ref):
    updated = below_ref[...] - ((p0[...] + p1[...]) + (p2[...] + p3[...]))
    out_ref[...] = dot3(split(updated), split(x_ref[...]), NT)


def swap(x, axis, size, step):
    return lax.ppermute(x, axis, [(i, i ^ step) for i in range(size)])


def tree(a, b, c, d):
    return (a + b) + (c + d)


def sum_near(x, rows_n, near_n):
    half = rows_n // 2

    def move(source):
        pairs = []
        for r in range(rows_n):
            z, rest = divmod(r, half)
            for n in range(near_n):
                m, w = source(n, z)
                pairs.append(((w * half + rest) * near_n + m % near_n, r * near_n + n))
        return lax.ppermute(x, ("rows", "near"), pairs)

    far_off = move(lambda n, z: (n + 2, 1 - z))
    next_1 = move(lambda n, z: (n + 2 * z - 1, 1 - z))
    next_2 = move(lambda n, z: (n + 1 - 2 * z, z))
    return (x + far_off) + (next_1 + next_2)


def body(sizes, diag_block, history_rows, panel_below, history_below):
    rows_n, near_n, far_n = sizes
    panel = diag_block.shape[0]
    mine, depth = history_rows.shape
    share = panel_below.shape[0]
    place = lax.axis_index("rows")
    me = place.reshape(1)
    at = jnp.stack([lax.axis_index("near"), lax.axis_index("far")])
    core = lambda x: swap(x, "rows", rows_n, 1)
    along_y = lambda x, k: swap(x, "rows", rows_n, 2 * k)
    other_z = swap(history_rows, "rows", rows_n, 8)
    low = place < rows_n // 2
    pair = jnp.concatenate([jnp.where(low, history_rows, other_z), jnp.where(low, other_z, history_rows)], 0)
    y1, y3 = along_y(pair, 1), along_y(pair, 3)
    close = [pair, y1, y3]
    close_other = [core(x) for x in close]
    gathered = jax.ShapeDtypeStruct((panel, depth), BF16)
    schur_part, hi, lo = call(
        schur_kernel,
        (jax.ShapeDtypeStruct((2 * mine, panel), F32), gathered, gathered),
        [SMEM] + [VMEM] * 6,
        [me] + close + close_other,
        flops=24 * mine * depth * panel,
        moved=8 * panel * depth,
    )
    y2 = [along_y(y3[:mine], 1), along_y(y1[mine:], 3)]
    *y2_late, _ = lax.optimization_barrier((*y2, schur_part))
    by_far = [swap(schur_part, "far", far_n, k) for k in (1, 2, 3)]
    hi, lo = call(
        complete_kernel,
        (gathered, gathered),
        [SMEM] + [VMEM] * 6,
        [me] + y2_late + [core(x) for x in y2_late] + [hi, lo],
        moved=2 * panel * depth,
        aliases=((5, 0), (6, 1)),
    )
    below = history_below.reshape(near_n, far_n, share, depth)
    a_send, b_send, a_keep, b_keep = products(at, below, hi, lo)
    *by_far, a_send, b_send = lax.optimization_barrier((*by_far, a_send, b_send))
    schur_part = tree(schur_part, *by_far)
    schur_part = sum_near(schur_part, rows_n, near_n)
    schur_pieces = [schur_part] + [along_y(schur_part, k) for k in (1, 2, 3)]
    schur_pieces = schur_pieces + [core(x) for x in schur_pieces]
    a_got, b_got = swap(a_send, "far", far_n, 1), swap(b_send, "far", far_n, 3)
    block = jax.ShapeDtypeStruct(a_send.shape[1:], F32)
    a_next, b_next = call(middle_kernel, (block, block), [VMEM] * 4, [a_keep, a_got, b_keep, b_got], moved=2**20)
    a_last, b_last = swap(a_next, "far", far_n, 3), swap(b_next, "far", far_n, 1)
    sums = call(
        combine_kernel,
        (jax.ShapeDtypeStruct((share, panel), F32),) * near_n,
        [VMEM] * 6,
        [a_keep, a_got, a_last, b_keep, b_got, b_last],
        moved=2**20,
    )
    sums = [sums[0]] + [swap(sums[j], "near", near_n, j) for j in (1, 2, 3)]
    square = jax.ShapeDtypeStruct((panel, panel), F32)
    diag_factor, inverse = call(
        cholesky_kernel,
        (square,) * 2,
        [SMEM] + [VMEM] * 9,
        [me, diag_block] + schur_pieces,
        scratch=[pltpu.VMEM((panel, panel), F32), pltpu.VMEM((2, 10, 8, 128), F32)],
        flops=120 * panel**3,
        moved=16 * panel * panel,
    )
    panel_factor = call(
        final_kernel,
        jax.ShapeDtypeStruct((share, panel), F32),
        [VMEM] * 6,
        [panel_below] + sums + [inverse],
        flops=6 * share * panel * panel,
        moved=8 * panel * panel,
    )
    return (panel_factor, diag_factor)


def solution(mesh):
    sizes = tuple(mesh.shape[name] for name in ("rows", "near", "far"))
    return jax.shard_map(
        functools.partial(body, sizes),
        mesh=mesh,
        in_specs=(
            P(),
            P("rows", ("near", "far")),
            P(("rows", "near", "far"), None),
            P("rows", ("near", "far")),
        ),
        out_specs=(P(("rows", "near", "far"), None), P()),
        check_vma=False,
    )
```

```python
import functools

import jax
import jax.numpy as jnp
from jax import lax
from jax.experimental import pallas as pl
from jax.experimental.pallas import tpu as pltpu
from jax.sharding import PartitionSpec as P

F32, BF16 = jnp.float32, jnp.bfloat16
NT = (((1,), (1,)), ((), ()))
NN = (((1,), (0,)), ((), ()))
VMEM = pl.BlockSpec(memory_space=pltpu.VMEM)
SMEM = pl.BlockSpec(memory_space=pltpu.SMEM)
PRODUCT_VMEM = 45


def split(x):
    hi = x.astype(BF16)
    return hi, (x - hi.astype(F32)).astype(BF16)


def dot3(a, b, dims):
    d = lambda x, y: lax.dot_general(x, y, dims, preferred_element_type=F32)
    return d(a[0], b[1]) + d(a[1], b[0]) + d(a[0], b[0])


def call(kernel, out_shape, in_specs, args, scratch=(), flops=0, moved=0, vmem=16, aliases=()):
    outs = jax.tree.map(lambda _: VMEM, out_shape)
    return pl.pallas_call(
        kernel,
        out_shape=out_shape,
        in_specs=in_specs,
        out_specs=outs,
        scratch_shapes=list(scratch),
        input_output_aliases=dict(aliases),
        cost_estimate=pl.CostEstimate(flops=flops, bytes_accessed=moved, transcendentals=0),
        compiler_params=pltpu.CompilerParams(vmem_limit_bytes=vmem * 2**20),
    )(*args)


def at_rows(me, z, y_step, core_step, size):
    place = z * 8 + lax.rem(me ^ (y_step * 2 + core_step), 8)
    return pl.ds(pl.multiple_of(place * size, size), size)


def slot_of(shape, size):
    return lax.rem(lax.broadcasted_iota(jnp.int32, shape, 1) // (2 * size), 4)


def join_kernel(me_ref, mine_ref, other_ref, out_ref):
    size = mine_ref.shape[0]
    z = me_ref[0] // 8
    out_ref[pl.ds(pl.multiple_of(z * size, size), size), :] = mine_ref[...]
    out_ref[pl.ds(pl.multiple_of((1 - z) * size, size), size), :] = other_ref[...]


def schur_kernel(me_ref, *refs):
    pieces, (out_ref, hi_ref, lo_ref) = refs[:6], refs[6:]
    me = me_ref[0]
    size = pieces[0].shape[0] // 2
    for core_step in range(2):
        for i, y_step in enumerate((0, 1, 3)):
            hi, lo = split(pieces[core_step * 3 + i][...])
            for z in range(2):
                part = slice(z * size, (z + 1) * size)
                for slot in (y_step, 2) if y_step == 3 else (y_step,):
                    at = at_rows(me, z, slot, core_step, size)
                    hi_ref[at, :] = hi[part]
                    lo_ref[at, :] = lo[part]
    left = split(jnp.concatenate([pieces[0][...], pieces[1][...]], 0))
    both = dot3(left, (hi_ref[...], lo_ref[...]), NT)
    here, near = both[:2 * size], both[2 * size:]
    y = lax.rem(me // 2, 4)
    out_ref[...] = jnp.where(slot_of(here.shape, size) == (y ^ 2), near, here)


def complete_kernel(me_ref, *refs):
    pieces, (hi_ref, lo_ref) = refs[:4], refs[6:]
    me = me_ref[0]
    size = pieces[0].shape[0]
    for core_step in range(2):
        for z in range(2):
            at = at_rows(me, z, 2, core_step, size)
            hi_ref[at, :], lo_ref[at, :] = split(pieces[core_step * 2 + z][...])


def split_kernel(x_ref, hi_ref, lo_ref):
    hi_ref[...], lo_ref[...] = split(x_ref[...])


def split_rows(x, block):
    rows, depth = x.shape
    spec = pl.BlockSpec((block, depth), lambda i: (i, 0))
    return pl.pallas_call(
        split_kernel,
        out_shape=(jax.ShapeDtypeStruct(x.shape, BF16),) * 2,
        grid=(rows // block,),
        in_specs=[spec],
        out_specs=(spec, spec),
        cost_estimate=pl.CostEstimate(flops=2 * x.size, bytes_accessed=8 * x.size, transcendentals=0),
        compiler_params=pltpu.CompilerParams(vmem_limit_bytes=56 * 2**20),
    )(x)


def long_dot(left_hi, left_lo, hi, lo):
    left = jnp.concatenate([left_hi, left_lo, left_hi], 1)
    right = jnp.concatenate([lo, hi, hi], 1)
    return lax.dot_general(left, right, NT, preferred_element_type=F32)


def product_kernel(at_ref, below_hi, below_lo, hi_ref, lo_ref, a_send, b_send, a_keep, b_keep, held_hi, held_lo, sems):
    near, far = at_ref[0], at_ref[1]
    near_n, _, share, _ = below_hi.shape
    half = a_send.shape[2]
    groups = ((1, 2), (3, 0))
    copies = {}
    for k in (1, 2, 3, 0):
        for j in range(near_n):
            for i, (source, held) in enumerate(((below_hi, held_hi), (below_lo, held_lo))):
                to = held.at[k, pl.ds(j * share, share)]
                copies[k, j, i] = pltpu.make_async_copy(source.at[near ^ j, far ^ k], to, sems.at[i, k, j])
                copies[k, j, i].start()
    places = {1: ((a_send, 0), (b_keep, 1)), 2: ((a_send, 1), (b_send, 1)),
              3: ((a_keep, 1), (b_send, 0)), 0: ((a_keep, 0), (b_keep, 0))}
    for group in groups:
        for k in group:
            for j in range(near_n):
                for i in range(2):
                    copies[k, j, i].wait()
        left = [jnp.concatenate([held[k] for k in group], 0) for held in (held_hi, held_lo)]
        out = long_dot(*left, hi_ref[...], lo_ref[...])
        size = out.shape[0] // 2
        for i, k in enumerate(group):
            (a, at_a), (b, at_b) = places[k]
            a[at_a] = out[i * size:(i + 1) * size, :half]
            b[at_b] = out[i * size:(i + 1) * size, half:]


def products(at, below, hi, lo):
    near_n, far_n, share, depth = below[0].shape
    panel = hi.shape[0]
    rows = near_n * share
    return call(
        product_kernel,
        (jax.ShapeDtypeStruct((2, rows, panel // 2), F32),) * 4,
        [SMEM] + [pl.BlockSpec(memory_space=pl.ANY)] * 2 + [VMEM] * 2,
        [at, *below, hi, lo],
        scratch=[pltpu.VMEM((far_n, rows, depth), BF16)] * 2 + [pltpu.SemaphoreType.DMA((2, far_n, near_n))],
        flops=9 * far_n * rows * depth * panel,
        moved=6 * 2**20,
        vmem=PRODUCT_VMEM,
    )


def middle_kernel(a_keep, a_got, b_keep, b_got, a_out, b_out):
    a_out[...] = a_keep[1] + a_got[1]
    b_out[...] = b_keep[1] + b_got[1]


def combine_kernel(a_keep, a_got, a_last, b_keep, b_got, b_last, *outs):
    share, panel = outs[0].shape
    for j, out in enumerate(outs):
        rows = slice(j * share, (j + 1) * share)
        out[:, :panel // 2] = a_keep[0, rows] + a_got[0, rows] + a_last[rows]
        out[:, panel // 2:] = b_keep[0, rows] + b_got[0, rows] + b_last[rows]


def recip(x):
    r = pl.reciprocal(x, approx=True)
    return r * (2.0 - x * r)


def factor_block(rows, nb, sc):
    groups = len(rows)
    lane = lax.broadcasted_iota(jnp.int32, (8, nb), 1)
    sub = lax.broadcasted_iota(jnp.int32, (8, nb), 0)
    rows = list(rows)
    inv = [jnp.where(lane == sub + 8 * g, 1.0, 0.0) for g in range(groups)]
    bc = lambda x, k: jnp.broadcast_to(x[k:k + 1, :], (8, nb))
    col = lambda g, t, k: jnp.broadcast_to(rows[g][:, 8 * t + k:8 * t + k + 1], (8, nb))

    def stack(parts):
        out = parts[7]
        for k in range(7):
            out = jnp.where(sub == k, parts[k], out)
        return out

    for t in range(groups):
        own = [col(t, t, k) for k in range(8)]
        p = t % 2
        for m in range(8):
            sc[p, m] = own[m]
        sc[p, 8] = rows[t]
        sc[p, 9] = inv[t]
        lb = lambda m, s: jnp.broadcast_to(sc[p, m, s:s + 1, :], (8, nb))
        e = [[lb(m, s) for m in range(s + 1)] for s in range(8)]
        u = [lb(8, k) for k in range(8)]
        v = [lb(9, k) for k in range(8)]
        diag, pairs = [], []
        for k in range(0, 8, 2):
            a, b, c = e[k][k], e[k + 1][k], e[k + 1][k + 1]
            det = a * c - b * b
            ra, rd = recip(a), recip(det)
            r1 = a * rd
            diag += [a, det * ra]
            low = b * ra
            u[k + 1] = u[k + 1] - low * u[k]
            v[k + 1] = v[k + 1] - low * v[k]
            for s in range(k + 2, 8):
                l0 = e[s][k] * ra
                e[s][k + 1] = e[s][k + 1] - l0 * b
                l1 = e[s][k + 1] * r1
                for m in range(k + 2, s + 1):
                    e[s][m] = (e[s][m] - l0 * e[m][k]) - l1 * e[m][k + 1]
                u[s] = (u[s] - l0 * u[k]) - l1 * u[k + 1]
                v[s] = (v[s] - l0 * v[k]) - l1 * v[k + 1]
            pairs.append((ra, r1))
        for g in range(t + 1, min(t + 1 + 3, groups)):
            f = [col(g, t, k) for k in range(8)]
            for k in range(0, 8, 2):
                ra, r1 = pairs[k // 2]
                f0 = f[k] * ra
                f1 = (f[k + 1] - f0 * e[k + 1][k]) * r1
                for m in range(k + 2, 8):
                    f[m] = (f[m] - f0 * e[m][k]) - f1 * e[m][k + 1]
                rows[g] = (rows[g] - f0 * u[k]) - f1 * u[k + 1]
                inv[g] = (inv[g] - f0 * v[k]) - f1 * v[k + 1]
        scale = lax.rsqrt(stack(diag))
        rows[t] = jnp.where(lane >= sub + 8 * t, stack(u) * scale, 0.0)
        inv[t] = stack(v) * scale
        if t + 1 + 3 < groups:
            both = jnp.concatenate([rows[t], inv[t]], 1)
            hi = both.astype(BF16).astype(F32)
            lo = both - hi
            left = jnp.concatenate([hi[:, :nb], lo[:, :nb], hi[:, :nb], lo[:, :nb]], 0).astype(BF16)
            right = jnp.concatenate([hi, hi, lo, lo], 0).astype(BF16)
            step = lax.dot_general(left, right, (((0,), (0,)), ((), ())), preferred_element_type=F32)
            for g in range(t + 1 + 3, groups):
                rows[g] = rows[g] - step[8 * g:8 * g + 8, :nb]
                inv[g] = inv[g] - step[8 * g:8 * g + 8, nb:]
    return rows, inv


def factor_columns(w_ref, l_ref, x_ref, sc_ref):
    n = w_ref.shape[0]
    nb = 128
    blk = lambda i: slice(i * nb, (i + 1) * nb)
    for b in range(n // nb):
        rows = [w_ref[b * nb + 8 * g:b * nb + 8 * g + 8, blk(b)] for g in range(nb // 8)]
        up, inv = factor_block(rows, nb, sc_ref)
        x11 = jnp.concatenate(inv, 0)
        l_ref[blk(b), blk(b)] = jnp.concatenate(up, 0).T
        x_ref[blk(b), blk(b)] = x11
        if (b + 1) * nb < n:
            rest = slice((b + 1) * nb, n)
            l21 = dot3(split(w_ref[rest, blk(b)]), split(x11), NT)
            l_ref[rest, blk(b)] = l21
            ls = split(l21)
            w_ref[rest, rest] = w_ref[rest, rest] - dot3(ls, ls, NT)
        if b > 0:
            done = slice(0, b * nb)
            t = dot3(split(l_ref[blk(b), done]), split(x_ref[done, done]), NN)
            x_ref[blk(b), done] = -dot3(split(x11), split(t), NN)


def cholesky_kernel(me_ref, diag_ref, *refs):
    pieces, (l_ref, x_ref, w_ref, sc_ref) = refs[:8], refs[8:]
    me = me_ref[0]
    size = pieces[0].shape[0] // 2
    y = lax.rem(me // 2, 4)
    for core_step in range(2):
        for y_step in range(4):
            own = pieces[core_step * 4 + y_step][...]
            other = pieces[core_step * 4 + (y_step ^ 1)][...]
            tiles = [other[:, i:i + 128] for i in range(0, other.shape[1], 128)]
            other = jnp.concatenate([pltpu.roll(t, 64, 1) for t in tiles], 1)
            whole = jnp.where(slot_of(own.shape, size) == (y ^ y_step ^ 2), other, own)
            for z in range(2):
                at = at_rows(me, z, y_step, core_step, size)
                w_ref[at, :] = diag_ref[at, :] - whole[z * size:(z + 1) * size]
    l_ref[...] = jnp.zeros_like(l_ref)
    x_ref[...] = jnp.zeros_like(x_ref)
    factor_columns(w_ref, l_ref, x_ref, sc_ref)


def final_kernel(below_ref, p0, p1, p2, p3, x_ref, out_ref):
    updated = below_ref[...] - ((p0[...] + p1[...]) + (p2[...] + p3[...]))
    out_ref[...] = dot3(split(updated), split(x_ref[...]), NT)


def swap(x, axis, size, step):
    return lax.ppermute(x, axis, [(i, i ^ step) for i in range(size)])


def tree(a, b, c, d):
    return (a + b) + (c + d)


def sum_near(x, rows_n, near_n):
    half = rows_n // 2

    def move(source):
        pairs = []
        for r in range(rows_n):
            z, rest = divmod(r, half)
            for n in range(near_n):
                m, w = source(n, z)
                pairs.append(((w * half + rest) * near_n + m % near_n, r * near_n + n))
        return lax.ppermute(x, ("rows", "near"), pairs)

    far_off = move(lambda n, z: (n + 2, 1 - z))
    next_1 = move(lambda n, z: (n + 2 * z - 1, 1 - z))
    next_2 = move(lambda n, z: (n + 1 - 2 * z, z))
    return (x + far_off) + (next_1 + next_2)


def body(sizes, diag_block, history_rows, panel_below, history_below):
    rows_n, near_n, far_n = sizes
    panel = diag_block.shape[0]
    mine, depth = history_rows.shape
    share = panel_below.shape[0]
    place = lax.axis_index("rows")
    me = place.reshape(1)
    at = jnp.stack([lax.axis_index("near"), lax.axis_index("far")])
    core = lambda x: swap(x, "rows", rows_n, 1)
    along_y = lambda x, k: swap(x, "rows", rows_n, 2 * k)
    other_z = swap(history_rows, "rows", rows_n, 8)
    below_parts = split_rows(history_below, 2 * share)
    other_z, *below_parts = lax.optimization_barrier((other_z, *below_parts))
    pair = call(
        join_kernel,
        jax.ShapeDtypeStruct((2 * mine, depth), F32),
        [SMEM] + [VMEM] * 2,
        [me, history_rows, other_z],
        moved=16 * mine * depth,
        vmem=4,
    )
    y1, y3 = along_y(pair, 1), along_y(pair, 3)
    close = [pair, y1, y3]
    close_other = [core(x) for x in close]
    gathered = jax.ShapeDtypeStruct((panel, depth), BF16)
    schur_part, hi, lo = call(
        schur_kernel,
        (jax.ShapeDtypeStruct((2 * mine, panel), F32), gathered, gathered),
        [SMEM] + [VMEM] * 6,
        [me] + close + close_other,
        flops=24 * mine * depth * panel,
        moved=8 * panel * depth,
    )
    y2 = [along_y(y3[:mine], 1), along_y(y1[mine:], 3)]
    *y2_late, _ = lax.optimization_barrier((*y2, schur_part))
    by_far = [swap(schur_part, "far", far_n, k) for k in (1, 2, 3)]
    hi, lo = call(
        complete_kernel,
        (gathered, gathered),
        [SMEM] + [VMEM] * 6,
        [me] + y2_late + [core(x) for x in y2_late] + [hi, lo],
        moved=2 * panel * depth,
        aliases=((5, 0), (6, 1)),
    )
    below = [x.reshape(near_n, far_n, share, depth) for x in below_parts]
    a_send, b_send, a_keep, b_keep = products(at, below, hi, lo)
    *by_far, a_send, b_send = lax.optimization_barrier((*by_far, a_send, b_send))
    schur_part = tree(schur_part, *by_far)
    schur_part = sum_near(schur_part, rows_n, near_n)
    schur_pieces = [schur_part] + [along_y(schur_part, k) for k in (1, 2, 3)]
    schur_pieces = schur_pieces + [core(x) for x in schur_pieces]
    a_got, b_got = swap(a_send, "far", far_n, 1), swap(b_send, "far", far_n, 3)
    block = jax.ShapeDtypeStruct(a_send.shape[1:], F32)
    a_next, b_next = call(middle_kernel, (block, block), [VMEM] * 4, [a_keep, a_got, b_keep, b_got], moved=2**20)
    a_last, b_last = swap(a_next, "far", far_n, 3), swap(b_next, "far", far_n, 1)
    sums = call(
        combine_kernel,
        (jax.ShapeDtypeStruct((share, panel), F32),) * near_n,
        [VMEM] * 6,
        [a_keep, a_got, a_last, b_keep, b_got, b_last],
        moved=2**20,
    )
    sums = [sums[0]] + [swap(sums[j], "near", near_n, j) for j in (1, 2, 3)]
    square = jax.ShapeDtypeStruct((panel, panel), F32)
    diag_factor, inverse = call(
        cholesky_kernel,
        (square,) * 2,
        [SMEM] + [VMEM] * 9,
        [me, diag_block] + schur_pieces,
        scratch=[pltpu.VMEM((panel, panel), F32), pltpu.VMEM((2, 10, 8, 128), F32)],
        flops=120 * panel**3,
        moved=16 * panel * panel,
    )
    panel_factor = call(
        final_kernel,
        jax.ShapeDtypeStruct((share, panel), F32),
        [VMEM] * 6,
        [panel_below] + sums + [inverse],
        flops=6 * share * panel * panel,
        moved=8 * panel * panel,
    )
    return (panel_factor, diag_factor)


def solution(mesh):
    sizes = tuple(mesh.shape[name] for name in ("rows", "near", "far"))
    return jax.shard_map(
        functools.partial(body, sizes),
        mesh=mesh,
        in_specs=(
            P(),
            P("rows", ("near", "far")),
            P(("rows", "near", "far"), None),
            P("rows", ("near", "far")),
        ),
        out_specs=(P(("rows", "near", "far"), None), P()),
        check_vma=False,
    )
```

```python
import functools

import jax
import jax.numpy as jnp
from jax import lax
from jax.experimental import pallas as pl
from jax.experimental.pallas import tpu as pltpu
from jax.sharding import PartitionSpec as P

F32, BF16 = jnp.float32, jnp.bfloat16
NT = (((1,), (1,)), ((), ()))
NN = (((1,), (0,)), ((), ()))
VMEM = pl.BlockSpec(memory_space=pltpu.VMEM)
SMEM = pl.BlockSpec(memory_space=pltpu.SMEM)
PRODUCT_VMEM = 45


def split(x):
    hi = x.astype(BF16)
    return hi, (x - hi.astype(F32)).astype(BF16)


def dot3(a, b, dims):
    d = lambda x, y: lax.dot_general(x, y, dims, preferred_element_type=F32)
    return d(a[0], b[1]) + d(a[1], b[0]) + d(a[0], b[0])


def call(kernel, out_shape, in_specs, args, scratch=(), flops=0, moved=0, vmem=16, aliases=()):
    outs = jax.tree.map(lambda _: VMEM, out_shape)
    return pl.pallas_call(
        kernel,
        out_shape=out_shape,
        in_specs=in_specs,
        out_specs=outs,
        scratch_shapes=list(scratch),
        input_output_aliases=dict(aliases),
        cost_estimate=pl.CostEstimate(flops=flops, bytes_accessed=moved, transcendentals=0),
        compiler_params=pltpu.CompilerParams(vmem_limit_bytes=vmem * 2**20),
    )(*args)


def at_rows(me, z, y_step, core_step, size):
    place = z * 8 + lax.rem(me ^ (y_step * 2 + core_step), 8)
    return pl.ds(pl.multiple_of(place * size, size), size)


def slot_of(shape, size):
    return lax.rem(lax.broadcasted_iota(jnp.int32, shape, 1) // (2 * size), 4)


def join_kernel(me_ref, mine_ref, other_ref, out_ref):
    size = mine_ref.shape[0]
    z = me_ref[0] // 8
    out_ref[pl.ds(pl.multiple_of(z * size, size), size), :] = mine_ref[...]
    out_ref[pl.ds(pl.multiple_of((1 - z) * size, size), size), :] = other_ref[...]


def schur_kernel(me_ref, *refs):
    pieces, (out_ref, hi_ref, lo_ref) = refs[:6], refs[6:]
    me = me_ref[0]
    size = pieces[0].shape[0] // 2
    for core_step in range(2):
        for i, y_step in enumerate((0, 1, 3)):
            hi, lo = split(pieces[core_step * 3 + i][...])
            for z in range(2):
                part = slice(z * size, (z + 1) * size)
                for slot in (y_step, 2) if y_step == 3 else (y_step,):
                    at = at_rows(me, z, slot, core_step, size)
                    hi_ref[at, :] = hi[part]
                    lo_ref[at, :] = lo[part]
    left = split(jnp.concatenate([pieces[0][...], pieces[1][...]], 0))
    both = dot3(left, (hi_ref[...], lo_ref[...]), NT)
    here, near = both[:2 * size], both[2 * size:]
    y = lax.rem(me // 2, 4)
    out_ref[...] = jnp.where(slot_of(here.shape, size) == (y ^ 2), near, here)


def complete_kernel(me_ref, *refs):
    pieces, (hi_ref, lo_ref) = refs[:4], refs[6:]
    me = me_ref[0]
    size = pieces[0].shape[0]
    for core_step in range(2):
        for z in range(2):
            at = at_rows(me, z, 2, core_step, size)
            hi_ref[at, :], lo_ref[at, :] = split(pieces[core_step * 2 + z][...])


def long_dot(rows, hi, lo):
    left_hi, left_lo = split(rows)
    left = jnp.concatenate([left_hi, left_lo, left_hi], 1)
    right = jnp.concatenate([lo, hi, hi], 1)
    return lax.dot_general(left, right, NT, preferred_element_type=F32)


def product_kernel(at_ref, below_ref, hi_ref, lo_ref, a_send, b_send, a_keep, b_keep, held, sems):
    near, far = at_ref[0], at_ref[1]
    near_n, _, share, _ = below_ref.shape
    half = a_send.shape[2]
    groups = ((1, 2), (3, 0))
    copies = {}
    for k in (1, 2, 3, 0):
        for j in range(near_n):
            to = held.at[k, pl.ds(j * share, share)]
            copies[k, j] = pltpu.make_async_copy(below_ref.at[near ^ j, far ^ k], to, sems.at[k, j])
            copies[k, j].start()
    places = {1: ((a_send, 0), (b_keep, 1)), 2: ((a_send, 1), (b_send, 1)),
              3: ((a_keep, 1), (b_send, 0)), 0: ((a_keep, 0), (b_keep, 0))}
    for group in groups:
        for k in group:
            for j in range(near_n):
                copies[k, j].wait()
        out = long_dot(jnp.concatenate([held[k] for k in group], 0), hi_ref[...], lo_ref[...])
        size = out.shape[0] // 2
        for i, k in enumerate(group):
            (a, at_a), (b, at_b) = places[k]
            a[at_a] = out[i * size:(i + 1) * size, :half]
            b[at_b] = out[i * size:(i + 1) * size, half:]


def products(at, below, hi, lo):
    near_n, far_n, share, depth = below.shape
    panel = hi.shape[0]
    rows = near_n * share
    return call(
        product_kernel,
        (jax.ShapeDtypeStruct((2, rows, panel // 2), F32),) * 4,
        [SMEM, pl.BlockSpec(memory_space=pl.ANY), VMEM, VMEM],
        [at, below, hi, lo],
        scratch=[pltpu.VMEM((far_n, rows, depth), F32), pltpu.SemaphoreType.DMA((far_n, near_n))],
        flops=9 * far_n * rows * depth * panel,
        moved=6 * 2**20,
        vmem=PRODUCT_VMEM,
    )


def middle_kernel(a_keep, a_got, b_keep, b_got, a_out, b_out):
    a_out[...] = a_keep[1] + a_got[1]
    b_out[...] = b_keep[1] + b_got[1]


def combine_kernel(a_keep, a_got, a_last, b_keep, b_got, b_last, *outs):
    share, panel = outs[0].shape
    for j, out in enumerate(outs):
        rows = slice(j * share, (j + 1) * share)
        out[:, :panel // 2] = a_keep[0, rows] + a_got[0, rows] + a_last[rows]
        out[:, panel // 2:] = b_keep[0, rows] + b_got[0, rows] + b_last[rows]


def recip(x):
    r = pl.reciprocal(x, approx=True)
    return r * (2.0 - x * r)


def factor_block(rows, nb, sc):
    groups = len(rows)
    lane = lax.broadcasted_iota(jnp.int32, (8, nb), 1)
    sub = lax.broadcasted_iota(jnp.int32, (8, nb), 0)
    rows = list(rows)
    inv = [jnp.where(lane == sub + 8 * g, 1.0, 0.0) for g in range(groups)]
    bc = lambda x, k: jnp.broadcast_to(x[k:k + 1, :], (8, nb))
    col = lambda g, t, k: jnp.broadcast_to(rows[g][:, 8 * t + k:8 * t + k + 1], (8, nb))

    def stack(parts):
        out = parts[7]
        for k in range(7):
            out = jnp.where(sub == k, parts[k], out)
        return out

    for t in range(groups):
        own = [col(t, t, k) for k in range(8)]
        p = t % 2
        for m in range(8):
            sc[p, m] = own[m]
        sc[p, 8] = rows[t]
        sc[p, 9] = inv[t]
        lb = lambda m, s: jnp.broadcast_to(sc[p, m, s:s + 1, :], (8, nb))
        e = [[lb(m, s) for m in range(s + 1)] for s in range(8)]
        u = [lb(8, k) for k in range(8)]
        v = [lb(9, k) for k in range(8)]
        diag, pairs = [], []
        for k in range(0, 8, 2):
            a, b, c = e[k][k], e[k + 1][k], e[k + 1][k + 1]
            det = a * c - b * b
            ra, rd = recip(a), recip(det)
            r1 = a * rd
            diag += [a, det * ra]
            low = b * ra
            u[k + 1] = u[k + 1] - low * u[k]
            v[k + 1] = v[k + 1] - low * v[k]
            for s in range(k + 2, 8):
                l0 = e[s][k] * ra
                e[s][k + 1] = e[s][k + 1] - l0 * b
                l1 = e[s][k + 1] * r1
                for m in range(k + 2, s + 1):
                    e[s][m] = (e[s][m] - l0 * e[m][k]) - l1 * e[m][k + 1]
                u[s] = (u[s] - l0 * u[k]) - l1 * u[k + 1]
                v[s] = (v[s] - l0 * v[k]) - l1 * v[k + 1]
            pairs.append((ra, r1))
        for g in range(t + 1, min(t + 1 + 3, groups)):
            f = [col(g, t, k) for k in range(8)]
            for k in range(0, 8, 2):
                ra, r1 = pairs[k // 2]
                f0 = f[k] * ra
                f1 = (f[k + 1] - f0 * e[k + 1][k]) * r1
                for m in range(k + 2, 8):
                    f[m] = (f[m] - f0 * e[m][k]) - f1 * e[m][k + 1]
                rows[g] = (rows[g] - f0 * u[k]) - f1 * u[k + 1]
                inv[g] = (inv[g] - f0 * v[k]) - f1 * v[k + 1]
        scale = lax.rsqrt(stack(diag))
        rows[t] = jnp.where(lane >= sub + 8 * t, stack(u) * scale, 0.0)
        inv[t] = stack(v) * scale
        if t + 1 + 3 < groups:
            both = jnp.concatenate([rows[t], inv[t]], 1)
            hi = both.astype(BF16).astype(F32)
            lo = both - hi
            left = jnp.concatenate([hi[:, :nb], lo[:, :nb], hi[:, :nb], lo[:, :nb]], 0).astype(BF16)
            right = jnp.concatenate([hi, hi, lo, lo], 0).astype(BF16)
            step = lax.dot_general(left, right, (((0,), (0,)), ((), ())), preferred_element_type=F32)
            for g in range(t + 1 + 3, groups):
                rows[g] = rows[g] - step[8 * g:8 * g + 8, :nb]
                inv[g] = inv[g] - step[8 * g:8 * g + 8, nb:]
    return rows, inv


def factor_columns(w_ref, l_ref, x_ref, sc_ref):
    n = w_ref.shape[0]
    nb = 128
    blk = lambda i: slice(i * nb, (i + 1) * nb)
    for b in range(n // nb):
        rows = [w_ref[b * nb + 8 * g:b * nb + 8 * g + 8, blk(b)] for g in range(nb // 8)]
        up, inv = factor_block(rows, nb, sc_ref)
        x11 = jnp.concatenate(inv, 0)
        l_ref[blk(b), blk(b)] = jnp.concatenate(up, 0).T
        x_ref[blk(b), blk(b)] = x11
        if (b + 1) * nb < n:
            rest = slice((b + 1) * nb, n)
            l21 = dot3(split(w_ref[rest, blk(b)]), split(x11), NT)
            l_ref[rest, blk(b)] = l21
            ls = split(l21)
            w_ref[rest, rest] = w_ref[rest, rest] - dot3(ls, ls, NT)
        if b > 0:
            done = slice(0, b * nb)
            t = dot3(split(l_ref[blk(b), done]), split(x_ref[done, done]), NN)
            x_ref[blk(b), done] = -dot3(split(x11), split(t), NN)


def cholesky_kernel(me_ref, diag_ref, *refs):
    pieces, (l_ref, x_ref, w_ref, sc_ref) = refs[:8], refs[8:]
    me = me_ref[0]
    size = pieces[0].shape[0] // 2
    y = lax.rem(me // 2, 4)
    for core_step in range(2):
        for y_step in range(4):
            own = pieces[core_step * 4 + y_step][...]
            other = pieces[core_step * 4 + (y_step ^ 1)][...]
            tiles = [other[:, i:i + 128] for i in range(0, other.shape[1], 128)]
            other = jnp.concatenate([pltpu.roll(t, 64, 1) for t in tiles], 1)
            whole = jnp.where(slot_of(own.shape, size) == (y ^ y_step ^ 2), other, own)
            for z in range(2):
                at = at_rows(me, z, y_step, core_step, size)
                w_ref[at, :] = diag_ref[at, :] - whole[z * size:(z + 1) * size]
    l_ref[...] = jnp.zeros_like(l_ref)
    x_ref[...] = jnp.zeros_like(x_ref)
    factor_columns(w_ref, l_ref, x_ref, sc_ref)


def final_kernel(below_ref, p0, p1, p2, p3, x_ref, out_ref):
    updated = below_ref[...] - ((p0[...] + p1[...]) + (p2[...] + p3[...]))
    out_ref[...] = dot3(split(updated), split(x_ref[...]), NT)


def swap(x, axis, size, step):
    return lax.ppermute(x, axis, [(i, i ^ step) for i in range(size)])


def tree(a, b, c, d):
    return (a + b) + (c + d)


def sum_near(x, rows_n, near_n):
    half = rows_n // 2

    def move(source):
        pairs = []
        for r in range(rows_n):
            z, rest = divmod(r, half)
            for n in range(near_n):
                m, w = source(n, z)
                pairs.append(((w * half + rest) * near_n + m % near_n, r * near_n + n))
        return lax.ppermute(x, ("rows", "near"), pairs)

    far_off = move(lambda n, z: (n + 2, 1 - z))
    next_1 = move(lambda n, z: (n + 2 * z - 1, 1 - z))
    next_2 = move(lambda n, z: (n + 1 - 2 * z, z))
    return (x + far_off) + (next_1 + next_2)


def body(sizes, diag_block, history_rows, panel_below, history_below):
    rows_n, near_n, far_n = sizes
    panel = diag_block.shape[0]
    mine, depth = history_rows.shape
    share = panel_below.shape[0]
    place = lax.axis_index("rows")
    me = place.reshape(1)
    at = jnp.stack([lax.axis_index("near"), lax.axis_index("far")])
    core = lambda x: swap(x, "rows", rows_n, 1)
    along_y = lambda x, k: swap(x, "rows", rows_n, 2 * k)
    other_z = swap(history_rows, "rows", rows_n, 8)
    pair = call(
        join_kernel,
        jax.ShapeDtypeStruct((2 * mine, depth), F32),
        [SMEM] + [VMEM] * 2,
        [me, history_rows, other_z],
        moved=16 * mine * depth,
        vmem=4,
    )
    y1, y3 = along_y(pair, 1), along_y(pair, 3)
    close = [pair, y1, y3]
    close_other = [core(x) for x in close]
    gathered = jax.ShapeDtypeStruct((panel, depth), BF16)
    schur_part, hi, lo = call(
        schur_kernel,
        (jax.ShapeDtypeStruct((2 * mine, panel), F32), gathered, gathered),
        [SMEM] + [VMEM] * 6,
        [me] + close + close_other,
        flops=24 * mine * depth * panel,
        moved=8 * panel * depth,
    )
    y2 = [along_y(y3[:mine], 1), along_y(y1[mine:], 3)]
    *y2_late, _ = lax.optimization_barrier((*y2, schur_part))
    by_far = [swap(schur_part, "far", far_n, k) for k in (1, 2, 3)]
    hi, lo = call(
        complete_kernel,
        (gathered, gathered),
        [SMEM] + [VMEM] * 6,
        [me] + y2_late + [core(x) for x in y2_late] + [hi, lo],
        moved=2 * panel * depth,
        aliases=((5, 0), (6, 1)),
    )
    below = history_below.reshape(near_n, far_n, share, depth)
    a_send, b_send, a_keep, b_keep = products(at, below, hi, lo)
    *by_far, a_send, b_send = lax.optimization_barrier((*by_far, a_send, b_send))
    schur_part = tree(schur_part, *by_far)
    schur_part = sum_near(schur_part, rows_n, near_n)
    schur_pieces = [schur_part] + [along_y(schur_part, k) for k in (1, 2, 3)]
    schur_pieces = schur_pieces + [core(x) for x in schur_pieces]
    a_got, b_got = swap(a_send, "far", far_n, 1), swap(b_send, "far", far_n, 3)
    block = jax.ShapeDtypeStruct(a_send.shape[1:], F32)
    a_next, b_next = call(middle_kernel, (block, block), [VMEM] * 4, [a_keep, a_got, b_keep, b_got], moved=2**20)
    a_last, b_last = swap(a_next, "far", far_n, 3), swap(b_next, "far", far_n, 1)
    sums = call(
        combine_kernel,
        (jax.ShapeDtypeStruct((share, panel), F32),) * near_n,
        [VMEM] * 6,
        [a_keep, a_got, a_last, b_keep, b_got, b_last],
        moved=2**20,
    )
    sums = [sums[0]] + [swap(sums[j], "near", near_n, j) for j in (1, 2, 3)]
    square = jax.ShapeDtypeStruct((panel, panel), F32)
    diag_factor, inverse = call(
        cholesky_kernel,
        (square,) * 2,
        [SMEM] + [VMEM] * 9,
        [me, diag_block] + schur_pieces,
        scratch=[pltpu.VMEM((panel, panel), F32), pltpu.VMEM((2, 10, 8, 128), F32)],
        flops=120 * panel**3,
        moved=16 * panel * panel,
    )
    panel_factor = call(
        final_kernel,
        jax.ShapeDtypeStruct((share, panel), F32),
        [VMEM] * 6,
        [panel_below] + sums + [inverse],
        flops=6 * share * panel * panel,
        moved=8 * panel * panel,
    )
    return (panel_factor, diag_factor)


def solution(mesh):
    sizes = tuple(mesh.shape[name] for name in ("rows", "near", "far"))
    return jax.shard_map(
        functools.partial(body, sizes),
        mesh=mesh,
        in_specs=(
            P(),
            P("rows", ("near", "far")),
            P(("rows", "near", "far"), None),
            P("rows", ("near", "far")),
        ),
        out_specs=(P(("rows", "near", "far"), None), P()),
        check_vma=False,
    )
```
